32 devices in a mesh: feat: 8 (over y, x, core), grp: 4 (over z).
Axes of the slice: x: 2, y: 2, z: 4, core: 2. Of those that a mesh axis runs over, the one named last changes fastest.
Arguments:
- x_feat: bfloat16 [4, 128, 8192], P('grp', 'feat'), may hold values from -6 to 6
- place: int32 [4, 64], P('grp'), may hold values from 0 to 63, each once within a row
- adj_one: bfloat16 [4, 64, 4, 128, 128], P('grp'), may hold values from -0.25 to 0.25
- cols_one: int32 [4, 64, 4], P('grp'), may hold values from 0 to 63
- count_one: int32 [4, 64], P('grp'), may hold values from 1 to 4
- w_one: bfloat16 [2, 128, 256], P(None, 'feat'), may hold values from -0.5 to 0.5
- bias_one: bfloat16 [256], replicated, may hold values from -3 to 3
- adj_two: bfloat16 [4, 64, 8, 128, 128], P('grp', 'feat'), may hold values from -0.1875 to 0.1875
- cols_two: int32 [4, 64, 8], P('grp', 'feat'), may hold values from 0 to 63, as said below
- count_two: int32 [4, 64], P('grp', 'feat'), may hold values from 1 to 8
- w_two: bfloat16 [2, 256, 256], replicated, may hold values from -0.375 to 0.375
- cotangent: bfloat16 [4, 8192, 256], P('grp', 'feat'), may hold values from -0.03125 to 0.03125
Outputs:
- layer_out: bfloat16 [4, 8192, 256], P('grp', 'feat')
- grad_one: float32 [2, 128, 256], P(None, 'feat')
The draws below stay inside these ranges and needn't reach their ends.
Inputs may be any that keep to these rules, and one draw needn't show every extreme that they name: `cols_two`: among the entries of the 8 row tiles of one device, at most 8 name tiles of any one owner (owner = value // 8), and no two name the same tile; in every group some owner is named exactly 8 times by every device. `place`: each row is a permutation of the group's row tiles.
All inputs are finite; a program needn't handle non-finite values.
Results may differ from the reference program's by a relative error of at most 0.0056.
Values may be sent and summed in bfloat16 or wider, within the bound.
No kernel may reach another device: no remote copies, remote signals or barrier semaphores. Data moves between devices by JAX's collectives and lax.ppermute only.
A program may use at most 128 MiB of HBM per device.

```python
import jax
import jax.numpy as jnp
from jax import lax

F = 128
HID = 256
TILE = 128
NEIGH_ONE = 4
NEIGH_TWO = 8
TILES_DEV = 8
GROUPS = 4
GROUP_TILES = 64
GROUP_ROWS = 8192
CAP = 8


def draw_cols_two(key, part):
    key = jax.random.fold_in(key, 11)
    owner_count = GROUP_TILES // TILES_DEV
    entries = TILES_DEV * NEIGH_TWO
    key_list = jax.random.split(key, 4)
    target = jax.random.randint(key_list[0], (GROUPS, 1, 1), 0, owner_count)
    rank_scores = jax.random.randint(key_list[1], (GROUPS, owner_count, owner_count), 0, 1 << 20) * owner_count + jnp.arange(owner_count)
    rank_scores = jnp.where(jnp.arange(owner_count)[None, None, :] == target, -1, rank_scores)
    order_list = jnp.argsort(rank_scores, axis=-1)
    pos_scores = jax.random.randint(key_list[2], (GROUPS, owner_count, entries), 0, 1 << 20) * entries + jnp.arange(entries)
    position = jnp.argsort(pos_scores, axis=-1)
    bundle = position // CAP
    owner_ids = jnp.take_along_axis(order_list, bundle, axis=-1)
    slot_scores = jax.random.randint(key_list[3], (GROUPS, owner_count, owner_count, TILES_DEV), 0, 1 << 20) * TILES_DEV + jnp.arange(TILES_DEV)
    slot_order = jnp.argsort(slot_scores, axis=-1).reshape(GROUPS, owner_count, owner_count * TILES_DEV)
    slot_ids = jnp.take_along_axis(slot_order, bundle * TILES_DEV + position % CAP, axis=-1)
    columns = owner_ids * TILES_DEV + slot_ids
    return columns.reshape(GROUPS, GROUP_TILES, NEIGH_TWO).astype(jnp.int32)


def place_ends(array, key, least, top_value):
    extent = array.shape
    spot = [jax.random.randint(jax.random.fold_in(key, axis), (), 0, extent[axis]) for axis in range(len(extent))]
    array = array.at[tuple(spot)].set(least)
    longest = extent.index(max(extent))
    spot[longest] = (spot[longest] + 1) % extent[longest]
    return array.at[tuple(spot)].set(top_value)


def level_of(key, extent, cuts, least, high):
    gain, own = 1.0, jax.random.fold_in(key, 6)
    for axis_at, blocks in cuts:
        heights = jnp.exp(jax.random.uniform(jax.random.fold_in(own, axis_at), (blocks,), jnp.float32, least / len(cuts), high / len(cuts)))
        gain = gain * jnp.repeat(heights, extent[axis_at] // blocks).reshape([-1 if axis == axis_at else 1 for axis in range(len(extent))])
    return gain


def gaussian(rng, dims, scale, most, cuts=(), kind=jnp.bfloat16):
    drawn = jax.random.normal(rng, dims, jnp.float32) * scale
    if len(cuts) > 0:
        drawn = level_of(rng, dims, cuts, -0.22, 0.18) * drawn
    return jnp.clip(drawn, min=-most, max=most).astype(kind)


def setup_inputs(seed: int = 0) -> dict:
    key_of = jax.random.split(jax.random.key(seed), 13)
    x_feat = gaussian(key_of[0], (GROUPS, F, GROUP_ROWS), 1.0, 6.0, ((0, 4), (1, 8)))
    place = jax.vmap(lambda own: jax.random.permutation(own, GROUP_TILES))(jax.random.split(key_of[1], GROUPS)).reshape((GROUPS, GROUP_TILES)).astype(jnp.int32)
    adj_one = gaussian(key_of[2], (GROUPS, GROUP_TILES, NEIGH_ONE, TILE, TILE), (TILE * NEIGH_ONE) ** -0.5, 0.25, ((0, 4),))
    cols_one = place_ends(jax.random.randint(key_of[3], (GROUPS, GROUP_TILES, NEIGH_ONE), 0, GROUP_TILES), jax.random.fold_in(key_of[3], 1), 0, GROUP_TILES - 1).astype(jnp.int32)
    count_one = place_ends(jax.random.randint(key_of[4], (GROUPS, GROUP_TILES), 1, NEIGH_ONE + 1), jax.random.fold_in(key_of[4], 1), 1, NEIGH_ONE).astype(jnp.int32)
    w_one = gaussian(key_of[5], (2, F, HID), F ** -0.5, 0.5, ((1, 8),))
    bias_one = gaussian(key_of[6], (HID,), 0.5, 3.0)
    adj_two = gaussian(key_of[7], (GROUPS, GROUP_TILES, NEIGH_TWO, TILE, TILE), (TILE * NEIGH_TWO) ** -0.5, 0.1875, ((0, 4), (1, 8)))
    cols_two = draw_cols_two(jax.random.fold_in(key_of[12], 71), 0)
    count_two = place_ends(jax.random.randint(key_of[9], (GROUPS, GROUP_TILES), 1, NEIGH_TWO + 1), jax.random.fold_in(key_of[9], 1), 1, NEIGH_TWO).astype(jnp.int32)
    w_two = gaussian(key_of[10], (2, HID, HID), HID ** -0.5, 0.375)
    cotangent = gaussian(key_of[11], (GROUPS, GROUP_ROWS, HID), (GROUPS * GROUP_ROWS) ** -0.5, 0.03125, ((0, 4), (1, 8)))
    return dict(x_feat=x_feat, place=place, adj_one=adj_one, cols_one=cols_one, count_one=count_one, w_one=w_one, bias_one=bias_one, adj_two=adj_two, cols_two=cols_two, count_two=count_two, w_two=w_two, cotangent=cotangent)


def reference(x_feat, place, adj_one, cols_one, count_one, w_one, bias_one, adj_two, cols_two, count_two, w_two, cotangent):
    def group_step(inputs):
        x_trans, placed, adj_a, cols_a, count_a, adj_b, cols_b, count_b, cot_rows = inputs
        x_rows = x_trans.T
        x_tiles = x_rows.reshape(GROUP_TILES, TILE, F)
        live_one = (jnp.arange(NEIGH_ONE)[None, :] < count_a[:, None]).astype(jnp.float32)
        adj_first = adj_a.astype(jnp.float32) * live_one[:, :, None, None]
        agg_one = jnp.einsum("tkij,tkjf->tif", adj_first, x_tiles[cols_a].astype(jnp.float32))
        agg_one = agg_one.astype(jnp.bfloat16).reshape(GROUP_ROWS, F)
        z_node = jnp.dot(x_rows, w_one[0], preferred_element_type=jnp.float32)
        z_node = z_node + jnp.dot(agg_one, w_one[1], preferred_element_type=jnp.float32)
        z_node = z_node + bias_one.astype(jnp.float32)
        inverse = jnp.zeros((GROUP_TILES,), jnp.int32).at[placed].set(jnp.arange(GROUP_TILES, dtype=jnp.int32))
        z_one = z_node.reshape(GROUP_TILES, TILE, HID)[inverse].reshape(GROUP_ROWS, HID)
        h_one = jax.nn.silu(z_one).astype(jnp.bfloat16)
        h_tiles = h_one.reshape(GROUP_TILES, TILE, HID)
        live_two = (jnp.arange(NEIGH_TWO)[None, :] < count_b[:, None]).astype(jnp.float32)
        adj_second = adj_b.astype(jnp.float32) * live_two[:, :, None, None]
        agg_two = jnp.einsum("tkij,tkjh->tih", adj_second, h_tiles[cols_b].astype(jnp.float32))
        agg_two = agg_two.astype(jnp.bfloat16).reshape(GROUP_ROWS, HID)
        out_rows = jnp.dot(h_one, w_two[0], preferred_element_type=jnp.float32)
        out_rows = (out_rows + jnp.dot(agg_two, w_two[1], preferred_element_type=jnp.float32)).astype(jnp.bfloat16)
        back_self = jnp.dot(cot_rows, w_two[0].T, preferred_element_type=jnp.float32)
        back_neigh = jnp.dot(cot_rows, w_two[1].T, preferred_element_type=jnp.float32).astype(jnp.bfloat16)
        terms = jnp.einsum("tkji,tjh->tkih", adj_second, back_neigh.reshape(GROUP_TILES, TILE, HID).astype(jnp.float32))
        terms = terms.astype(jnp.bfloat16)
        spread = jnp.zeros((GROUP_TILES, TILE, HID), jnp.float32).at[cols_b].add(terms.astype(jnp.float32))
        d_hidden = back_self + spread.reshape(GROUP_ROWS, HID)
        sigmoid_z = jax.nn.sigmoid(z_one)
        d_pre = (d_hidden * sigmoid_z * (1.0 + z_one * (1.0 - sigmoid_z))).astype(jnp.bfloat16)
        d_node = d_pre.reshape(GROUP_TILES, TILE, HID)[placed].reshape(GROUP_ROWS, HID)
        grads = jnp.stack([jnp.dot(x_trans, d_node, preferred_element_type=jnp.float32),
                           jnp.dot(agg_one.T, d_node, preferred_element_type=jnp.float32)])
        return out_rows, grads

    outs, grads = lax.map(group_step, (x_feat, place, adj_one, cols_one, count_one, adj_two, cols_two, count_two, cotangent))
    return outs, jnp.sum(grads, axis=0)
```

```python
import functools

import jax
import jax.numpy as jnp
from jax import lax
from jax.experimental import pallas as pl
from jax.experimental.pallas import tpu as pltpu
from jax.sharding import PartitionSpec as P

BATCH = 4
NT = (((1,), (1,)), ((), ()))
TN = (((0,), (0,)), ((), ()))
VMEM = pl.BlockSpec(memory_space=pltpu.VMEM)
SMEM = pl.BlockSpec(memory_space=pltpu.SMEM)
ANY = pl.BlockSpec(memory_space=pl.ANY)


def dot(a, b, dims=None):
    if dims is None:
        dims = (((1,), (0,)), ((), ()))
    return lax.dot_general(a, b, dims, preferred_element_type=jnp.float32)


def exchange(array, axis, mask):
    size = lax.axis_size(axis)
    return lax.ppermute(array, axis, [(i, i ^ mask) for i in range(size)])


def terms_kernel(
    dense, slots, me_ref, place_ref, cols_ref, count_ref, adj_ref, w_ref, cot_ref,
    d_ref, tile_list, slot_list, info, inverse, active,
):
    own, fan, tile, _ = adj_ref.shape
    hidden = w_ref.shape[-1]
    group_tiles = place_ref.shape[0]
    entries = own * fan
    padded = tile_list.shape[0]
    first = me_ref[0] * own
    own_slot = first if dense else entries

    @pl.loop(0, group_tiles)
    def _(t):
        inverse[place_ref[t]] = t

    @pl.loop(0, slots)
    def _(s):
        active[s] = 0

    @pl.loop(0, own)
    def _(p):
        active[own_slot + p] = 1
        d_ref[own_slot + p] = jnp.zeros((hidden, tile), d_ref.dtype)

        @pl.loop(0, fan)
        def _(k):
            @pl.when(k < count_ref[p])
            def _():
                e = p * fan + k
                active[cols_ref[e] if dense else e] = 1

    def visit(s, n):
        live = active[s] == 1

        @pl.when(live)
        def _():
            if dense:
                placed = s
            else:
                placed = jnp.where(s < entries, cols_ref[jnp.minimum(s, entries - 1)], first + s - entries)
            tile_list[n] = inverse[placed]
            slot_list[n] = s

        return n + live.astype(jnp.int32)

    n = lax.fori_loop(0, slots, visit, jnp.int32(0))
    info[0] = n

    @pl.loop(n, padded)
    def _(i):
        tile_list[i] = 0
        slot_list[i] = slots + lax.rem(i, BATCH)

    for b in range(BATCH):
        d_ref[slots + b] = jnp.zeros((hidden, tile), d_ref.dtype)

    @pl.loop(0, own)
    def _(p):
        cot = cot_ref[p]
        back = dot(w_ref[1], cot, NT).astype(jnp.bfloat16)
        for k in range(fan):
            e = p * fan + k
            live = (k < count_ref[p]).astype(jnp.float32)
            term = dot(back, adj_ref[p, k]) * live
            d_ref[cols_ref[e] if dense else e] = term.astype(d_ref.dtype)

    @pl.loop(0, own)
    def _(p):
        back = dot(w_ref[0], cot_ref[p], NT)
        d_ref[own_slot + p] = (back + d_ref[own_slot + p].astype(jnp.float32)).astype(d_ref.dtype)


def layer_one_kernel(
    blocks, slots, tile_list, slot_list, info, cols_ref, count_ref, *refs
):
    x_refs = refs[:blocks]
    bias_ref, adj_ref, d_ref, even_ref, odd_ref, h_ref = refs[blocks : blocks + 6]
    adj_buf, d_buf, h_buf, weight, bias, total, adj_sem, d_sem, h_sem = refs[blocks + 6 :]
    _, fan, tile, _ = adj_ref.shape
    hidden = bias_ref.shape[0]
    rows = x_refs[0].shape[0]
    features = rows * blocks
    columns = x_refs[0].shape[1]
    group_tiles = (columns - 2 * hidden - tile) // tile
    zero_tile = columns // tile - 1
    n_steps = (info[0] + BATCH - 1) // BATCH

    def adj_copy(i):
        return pltpu.make_async_copy(adj_ref.at[tile_list[i]], adj_buf.at[i], adj_sem.at[i])

    def d_copy(i):
        return pltpu.make_async_copy(d_ref.at[slot_list[i]], d_buf.at[i], d_sem.at[i])

    def h_copy(i):
        return pltpu.make_async_copy(h_buf.at[i], h_ref.at[slot_list[i]], h_sem.at[i])

    @pl.loop(0, n_steps * BATCH)
    def _(i):
        adj_copy(i).start()
        d_copy(i).start()

    def x_tile(t):
        at = pl.ds(pl.multiple_of(t * tile, tile), tile)
        return jnp.concatenate([x[:, at] for x in x_refs], axis=0)

    for part in range(2):
        at = pl.ds(group_tiles * tile + part * hidden, hidden)
        w = jnp.concatenate([x[:, at] for x in x_refs], axis=0)
        weight[:, part * features : (part + 1) * features] = w.astype(jnp.float32).T.astype(jnp.bfloat16)
    bias[...] = jnp.broadcast_to(bias_ref[...], bias.shape)
    total[...] = jnp.zeros_like(total)

    @pl.loop(0, n_steps)
    def _(step):
        both, downs = [], []
        for b in range(BATCH):
            i = step * BATCH + b
            t = tile_list[i]
            adj_copy(i).wait()
            agg = None
            for k in range(0, fan, 2):
                x_pair, a_pair = [], []
                for j in range(k, min(k + 2, fan)):
                    column = jnp.where(j < count_ref[t], cols_ref[t * fan + j], zero_tile)
                    x_pair.append(x_tile(column))
                    a_pair.append(adj_buf[i, j])
                piece = dot(jnp.concatenate(x_pair, axis=1), jnp.concatenate(a_pair, axis=1), NT)
                agg = piece if agg is None else agg + piece
            both.append(jnp.concatenate([x_tile(t), agg.astype(jnp.bfloat16)], axis=0))
        for b in range(0, BATCH, 2):
            pair = jnp.concatenate(both[b : b + 2], axis=1)
            z = dot(weight[...], pair) + bias[...]
            s = 0.5 * jnp.tanh(0.5 * z) + 0.5
            h = z * s
            slope = s + h * (1.0 - s)
            h = h.astype(jnp.bfloat16)
            for c in range(2):
                i = step * BATCH + b + c
                h_buf[i] = h[:, c * tile : (c + 1) * tile]
                h_copy(i).start()
                d_copy(i).wait()
                down = d_buf[i].astype(jnp.float32) * slope[:, c * tile : (c + 1) * tile]
                downs.append(down.astype(jnp.bfloat16))
        total[...] += dot(jnp.concatenate(both, axis=1), jnp.concatenate(downs, axis=1), NT)

    for m in range(even_ref.shape[0] * 2):
        out = even_ref if m % 2 == 0 else odd_ref
        share = features // (even_ref.shape[0] * 2)
        for part in range(2):
            at = part * features + m * share
            out[m // 2, part] = total[at : at + share]

    @pl.loop(0, n_steps * BATCH)
    def _(i):
        h_copy(i).wait()


def layer_two_kernel(
    dense, me_ref, cols_ref, count_ref, h_ref, adj_ref, w_ref, out_ref, h_buf, own_buf, h_sem, own_sem
):
    own, fan, tile, _ = adj_ref.shape
    hidden = w_ref.shape[-1]
    entries = own * fan
    own_slot = me_ref[0] * own if dense else entries

    def h_copy(p, k):
        e = p * fan + k
        slot = cols_ref[e] if dense else e
        return pltpu.make_async_copy(h_ref.at[slot], h_buf.at[e], h_sem.at[e])

    def own_copy(p):
        return pltpu.make_async_copy(h_ref.at[own_slot + p], own_buf.at[p], own_sem.at[p])

    @pl.loop(0, own)
    def _(p):
        own_copy(p).start()

        @pl.loop(0, fan)
        def _(k):
            live = k < count_ref[p]

            @pl.when(live)
            def _():
                h_copy(p, k).start()

            @pl.when(jnp.logical_not(live))
            def _():
                h_buf[p * fan + k] = jnp.zeros((hidden, tile), h_buf.dtype)

    @pl.loop(0, own)
    def _(p):
        own_copy(p).wait()

        @pl.loop(0, fan)
        def _(k):
            @pl.when(k < count_ref[p])
            def _():
                h_copy(p, k).wait()

        agg = None
        for k in range(0, fan, 2):
            pair = range(k, min(k + 2, fan))
            h_pair = jnp.concatenate([h_buf[p * fan + j] for j in pair], axis=1)
            a_pair = jnp.concatenate([adj_ref[p, j] for j in pair], axis=1)
            piece = dot(h_pair, a_pair, NT)
            agg = piece if agg is None else agg + piece
        out = dot(own_buf[p], w_ref[0], TN) + dot(agg.astype(jnp.bfloat16), w_ref[1], TN)
        out_ref[p] = out.astype(out_ref.dtype)


def body(
    x_feat,
    place,
    adj_one,
    cols_one,
    count_one,
    w_one,
    bias_one,
    adj_two,
    cols_two,
    count_two,
    w_two,
    cotangent,
):
    x_local = x_feat[0]
    feat_dev, group_rows = x_local.shape
    tile = adj_one.shape[-1]
    group_tiles = place.shape[1]
    fan_one = adj_one.shape[2]
    own, fan_two = adj_two.shape[1:3]
    hidden = w_two.shape[-1]
    feat_count = lax.axis_size("feat")
    features = feat_dev * feat_count
    entries = own * fan_two
    dense = entries == group_tiles
    slots = group_tiles if dense else entries + own
    padded = -(-slots // BATCH) * BATCH
    me = lax.axis_index("feat").astype(jnp.int32).reshape(1)

    packed = jnp.concatenate(
        [x_local, w_one[0], w_one[1], jnp.zeros((feat_dev, tile), x_local.dtype)], axis=1
    )
    near = [packed] + [exchange(packed, "feat", m) for m in range(2, feat_count, 2)]
    far = [exchange(block, "feat", 1) for block in near]
    gathered = [block for pair in zip(near, far) for block in pair]
    merge = max(1, 16 // feat_dev)
    if merge > 1:
        gathered = [
            jnp.concatenate(gathered[i : i + merge], axis=0) for i in range(0, feat_count, merge)
        ]
    blocks = len(gathered)

    flat_cols = cols_two[0].reshape(-1)
    cot = cotangent[0].reshape(own, tile, hidden)
    ints = functools.partial(jax.ShapeDtypeStruct, dtype=jnp.int32)
    down, tile_list, slot_list, info = pl.pallas_call(
        functools.partial(terms_kernel, dense, slots),
        out_shape=(
            jax.ShapeDtypeStruct((slots + BATCH, hidden, tile), jnp.bfloat16),
            ints((padded,)),
            ints((padded,)),
            ints((1,)),
        ),
        in_specs=[SMEM] * 4 + [VMEM] * 3,
        out_specs=(VMEM, SMEM, SMEM, SMEM),
        scratch_shapes=[pltpu.SMEM((group_tiles,), jnp.int32), pltpu.SMEM((slots,), jnp.int32)],
        compiler_params=pltpu.CompilerParams(vmem_limit_bytes=24 << 20),
        cost_estimate=pl.CostEstimate(
            flops=2 * entries * tile * tile * hidden, bytes_accessed=8 << 20, transcendentals=0
        ),
        name="terms",
    )(me, place[0], flat_cols, count_two[0], adj_two[0], w_two, cot)

    half = feat_count // 2
    share = jax.ShapeDtypeStruct((half, 2, feat_dev, hidden), jnp.float32)
    even, odd, h_tiles = pl.pallas_call(
        functools.partial(layer_one_kernel, blocks, slots),
        out_shape=(share, share, jax.ShapeDtypeStruct((slots + BATCH, hidden, tile), jnp.bfloat16)),
        in_specs=[SMEM] * 5 + [VMEM] * (blocks + 1) + [ANY] * 2,
        out_specs=(VMEM, VMEM, ANY),
        scratch_shapes=[
            pltpu.VMEM((padded, fan_one, tile, tile), jnp.bfloat16),
            pltpu.VMEM((padded, hidden, tile), jnp.bfloat16),
            pltpu.VMEM((padded, hidden, tile), jnp.bfloat16),
            pltpu.VMEM((hidden, 2 * features), jnp.bfloat16),
            pltpu.VMEM((hidden, 2 * tile), jnp.float32),
            pltpu.VMEM((2 * features, hidden), jnp.float32),
            pltpu.SemaphoreType.DMA((padded,)),
            pltpu.SemaphoreType.DMA((padded,)),
            pltpu.SemaphoreType.DMA((padded,)),
        ],
        compiler_params=pltpu.CompilerParams(vmem_limit_bytes=48 << 20),
        cost_estimate=pl.CostEstimate(
            flops=2 * slots * tile * 2 * features * hidden * 3,
            bytes_accessed=20 << 20,
            transcendentals=slots * tile * hidden,
        ),
        name="layer_one",
    )(
        tile_list, slot_list, info, cols_one[0].reshape(-1), count_one[0], *gathered,
        bias_one.astype(jnp.float32).reshape(hidden, 1), adj_one[0], down,
    )

    layer_out = pl.pallas_call(
        functools.partial(layer_two_kernel, dense),
        out_shape=jax.ShapeDtypeStruct((own, tile, hidden), jnp.bfloat16),
        in_specs=[SMEM] * 3 + [ANY, VMEM, VMEM],
        out_specs=VMEM,
        scratch_shapes=[
            pltpu.VMEM((entries, hidden, tile), jnp.bfloat16),
            pltpu.VMEM((own, hidden, tile), jnp.bfloat16),
            pltpu.SemaphoreType.DMA((entries,)),
            pltpu.SemaphoreType.DMA((own,)),
        ],
        compiler_params=pltpu.CompilerParams(vmem_limit_bytes=24 << 20),
        cost_estimate=pl.CostEstimate(
            flops=2 * entries * tile * tile * hidden, bytes_accessed=8 << 20, transcendentals=0
        ),
        name="layer_two",
    )(me, flat_cols, count_two[0], h_tiles, adj_two[0], w_two)

    even = even + exchange(odd, "feat", 1)
    grad = even[0]
    for received in [exchange(even[j], "feat", 2 * j) for j in range(1, half)]:
        grad = grad + received
    level = [grad] + [exchange(grad, "grp", m) for m in range(1, lax.axis_size("grp"))]
    while len(level) > 1:
        level = [level[i] + level[i + 1] for i in range(0, len(level), 2)]
    return (layer_out.reshape(1, own * tile, hidden), level[0])


def solution(mesh):
    in_specs = (
        P("grp", "feat", None),
        P("grp", None),
        P("grp", None, None, None, None),
        P("grp", None, None),
        P("grp", None),
        P(None, "feat", None),
        P(),
        P("grp", "feat", None, None, None),
        P("grp", "feat", None),
        P("grp", "feat"),
        P(),
        P("grp", "feat", None),
    )
    out_specs = (P("grp", "feat", None), P(None, "feat", None))
    return jax.shard_map(body, mesh=mesh, in_specs=in_specs, out_specs=out_specs, check_vma=False)
```

```python
import functools

import jax
import jax.numpy as jnp
from jax import lax
from jax.experimental import pallas as pl
from jax.experimental.pallas import tpu as pltpu
from jax.sharding import PartitionSpec as P

BATCH = 4
HEAD = 8
NT = (((1,), (1,)), ((), ()))
TN = (((0,), (0,)), ((), ()))
VMEM = pl.BlockSpec(memory_space=pltpu.VMEM)
SMEM = pl.BlockSpec(memory_space=pltpu.SMEM)
HBM = pl.BlockSpec(memory_space=pltpu.HBM)


def dot(a, b, dims=(((1,), (0,)), ((), ()))):
    return lax.dot_general(a, b, dims, preferred_element_type=jnp.float32)


def exchange(array, axis, mask):
    size = lax.axis_size(axis)
    return lax.ppermute(array, axis, [(i, i ^ mask) for i in range(size)])


class Plan:
    def __init__(self, group_tiles, fan_one, own, fan_two, zero_tile):
        self.group_tiles, self.fan_one, self.own, self.fan_two = group_tiles, fan_one, own, fan_two
        self.entries = own * fan_two
        self.dense = self.entries == group_tiles
        self.slots = group_tiles if self.dense else self.entries + own
        self.steps = -(-self.slots // BATCH)
        self.padded = self.steps * BATCH
        self.place = 1
        self.cols_two = self.place + group_tiles
        self.count_two = self.cols_two + self.entries
        self.cols_one = self.count_two + own
        self.count_one = self.cols_one + group_tiles * fan_one
        self.tile_at = HEAD
        self.slot_at = self.tile_at + self.padded + BATCH
        self.column_at = self.slot_at + self.padded + BATCH
        self.entry_at = self.column_at + (self.padded + BATCH) * fan_one
        self.table = self.entry_at + self.entries
        self.zero_tile = zero_tile


def prepare_kernel(
    plan, ints, bias_ref, adj_one_ref, adj_two_ref, w_ref, cot_ref,
    d_ref, adj_one, adj_two, w_two, bias, table,
    cot, back, inverse, active, sems, adj_sems,
):
    own, fan, fan_one = plan.own, plan.fan_two, plan.fan_one
    tile = adj_two.shape[-1]
    hidden = w_two.shape[-1]
    first = ints[0] * own
    own_slot = first if plan.dense else plan.entries

    copies = [
        pltpu.make_async_copy(source, to, sems.at[i])
        for i, (source, to) in enumerate(((w_ref, w_two), (cot_ref, cot), (adj_two_ref, adj_two)))
    ]
    for copy in copies:
        copy.start()

    def adj_copy(i):
        t = table[plan.tile_at + i]
        return pltpu.make_async_copy(adj_one_ref.at[t], adj_one.at[i], adj_sems.at[i])

    @pl.loop(0, plan.group_tiles, unroll=8)
    def _(t):
        inverse[ints[plan.place + t]] = t

    @pl.loop(0, own)
    def _(p):
        count = ints[plan.count_two + p]
        for k in range(fan):
            e = p * fan + k
            slot = ints[plan.cols_two + e] if plan.dense else e
            live = k < count
            table[plan.entry_at + e] = jnp.where(live, slot, own_slot)
            if plan.dense:
                mine = jnp.logical_and(slot >= own_slot, slot < own_slot + own)
                live = jnp.logical_or(live, mine)
            active[slot] = live.astype(jnp.int32)
        if not plan.dense:
            active[plan.entries + p] = 1

    def visit(s, n):
        if plan.dense:
            placed = s
        else:
            named = ints[plan.cols_two + jnp.minimum(s, plan.entries - 1)]
            placed = jnp.where(s < plan.entries, named, first + s - plan.entries)
        table[plan.tile_at + n] = inverse[placed]
        table[plan.slot_at + n] = s
        return n + active[s]

    n = lax.fori_loop(0, plan.slots, visit, jnp.int32(0), unroll=8)
    steps = lax.div(n + BATCH - 1, BATCH)
    table[0] = steps
    table[1] = own_slot

    @pl.loop(n, plan.padded + BATCH)
    def _(i):
        table[plan.tile_at + i] = 0
        table[plan.slot_at + i] = plan.slots + lax.rem(i, BATCH)

    @pl.loop(0, steps + 1)
    def _(step):
        for b in range(BATCH):
            i = step * BATCH + b
            t = table[plan.tile_at + i]
            count = ints[plan.count_one + t]
            for k in range(fan_one):
                column = ints[plan.cols_one + t * fan_one + k]
                table[plan.column_at + i * fan_one + k] = jnp.where(k < count, column, plan.zero_tile)

    @pl.loop(0, steps)
    def _(step):
        for b in range(BATCH):
            adj_copy(step * BATCH + b).start()

    for b in range(BATCH):
        d_ref[plan.slots + b] = jnp.zeros((hidden, tile), d_ref.dtype)
    if not plan.dense:
        for p in range(own):
            d_ref[plan.entries + p] = jnp.zeros((hidden, tile), d_ref.dtype)
    bias[...] = jnp.broadcast_to(bias_ref[...], (tile, hidden)).T

    copies[0].wait()
    copies[1].wait()
    back[...] = dot(w_two[1], cot[...], NT).astype(back.dtype)
    copies[2].wait()

    @pl.loop(0, own)
    def _(p):
        @pl.loop(ints[plan.count_two + p], fan)
        def _(k):
            adj_two[p, k] = jnp.zeros((tile, tile), adj_two.dtype)

    for p in range(own):
        tiles = jnp.concatenate([adj_two[p, k] for k in range(fan)], axis=1)
        term = dot(back[:, p * tile : (p + 1) * tile], tiles).astype(d_ref.dtype)
        for k in range(fan):
            e = p * fan + k
            slot = ints[plan.cols_two + e] if plan.dense else e
            d_ref[slot] = term[:, k * tile : (k + 1) * tile]

    self_rows = dot(w_two[0], cot[...], NT)
    for p in range(own):
        mine = self_rows[:, p * tile : (p + 1) * tile] + d_ref[own_slot + p].astype(jnp.float32)
        d_ref[own_slot + p] = mine.astype(d_ref.dtype)

    @pl.loop(0, steps)
    def _(step):
        for b in range(BATCH):
            adj_copy(step * BATCH + b).wait()


def layer_one_kernel(plan, blocks, table, *refs):
    x_refs = refs[:blocks]
    bias, adj_one, d_ref, even_ref, odd_ref, h_ref, weight, total, both, downs = refs[blocks:]
    fan = plan.fan_one
    tile = adj_one.shape[-1]
    hidden = bias.shape[0]
    features = x_refs[0].shape[0] * blocks
    steps = table[0]

    def x_tile(t):
        at = pl.ds(pl.multiple_of(t * tile, tile), tile)
        return jnp.concatenate([x[:, at] for x in x_refs], axis=0)

    def lanes(b):
        return slice(b * tile, (b + 1) * tile)

    def aggregate(step):
        at = lax.rem(step, 2)
        for b in range(BATCH):
            i = step * BATCH + b
            j = jnp.minimum(i, plan.padded - 1)
            x_all = [x_tile(table[plan.column_at + i * fan + k]) for k in range(fan)]
            tiles = [adj_one[j, k] for k in range(fan)]
            agg = dot(jnp.concatenate(x_all, axis=1), jnp.concatenate(tiles, axis=1), NT)
            both[at, :features, lanes(b)] = x_tile(table[plan.tile_at + i])
            both[at, features:, lanes(b)] = agg.astype(both.dtype)

    def activate(step):
        at = lax.rem(step, 2)
        for b in range(0, BATCH, 2):
            z = dot(weight[...], both[at, :, b * tile : (b + 2) * tile])
            for c in range(2):
                v = z[:, lanes(c)] + bias[...]
                s = 0.5 * jnp.tanh(0.5 * v) + 0.5
                h = v * s
                slope = s + h * (1.0 - s)
                slot = table[plan.slot_at + step * BATCH + b + c]
                h_ref[slot] = h.astype(h_ref.dtype)
                down = d_ref[slot].astype(jnp.float32) * slope
                downs[at, :, lanes(b + c)] = down.astype(downs.dtype)

    def contract(step):
        at = lax.rem(step + 2, 2)
        total[...] += dot(both[at], downs[at], NT)

    for part in range(2):
        at = pl.ds(plan.group_tiles * tile + part * hidden, hidden)
        w = jnp.concatenate([x[:, at] for x in x_refs], axis=0)
        weight[:, part * features : (part + 1) * features] = w.astype(jnp.float32).T.astype(weight.dtype)
    total[...] = jnp.zeros_like(total)
    both[1] = jnp.zeros(both.shape[1:], both.dtype)
    downs[1] = jnp.zeros(downs.shape[1:], downs.dtype)
    aggregate(0)

    @pl.loop(0, steps)
    def _(step):
        contract(step - 1)
        activate(step)
        aggregate(step + 1)

    contract(steps - 1)
    half = even_ref.shape[0]
    share = features // (2 * half)
    for m in range(2 * half):
        out = even_ref if m % 2 == 0 else odd_ref
        for part in range(2):
            at = part * features + m * share
            out[m // 2, part] = total[at : at + share]


def layer_two_kernel(plan, table, h_ref, adj_two, w_ref, out_ref, agg, out, sems):
    own, fan = plan.own, plan.fan_two
    tile = adj_two.shape[-1]
    own_slot = table[1]
    for p in range(own):
        h_all = [h_ref[table[plan.entry_at + p * fan + k]] for k in range(fan)]
        tiles = [adj_two[p, k] for k in range(fan)]
        rows = dot(jnp.concatenate(h_all, axis=1), jnp.concatenate(tiles, axis=1), NT)
        agg[p] = rows.astype(agg.dtype)
    copies = []
    for p in range(own):
        rows = dot(h_ref[own_slot + p], w_ref[0], TN) + dot(agg[p], w_ref[1], TN)
        out[p] = rows.astype(out.dtype)
        copies.append(pltpu.make_async_copy(out.at[p], out_ref.at[p], sems.at[p]))
        copies[-1].start()
    for copy in copies:
        copy.wait()


def call_prepare(plan, ints, bias, adj_one, adj_two, w_two, cot):
    own, fan, tile, _ = adj_two.shape
    hidden = w_two.shape[-1]
    kind = adj_one.dtype
    return pl.pallas_call(
        functools.partial(prepare_kernel, plan),
        out_shape=(
            jax.ShapeDtypeStruct((plan.slots + BATCH, hidden, tile), kind),
            jax.ShapeDtypeStruct((plan.padded, plan.fan_one, tile, tile), kind),
            jax.ShapeDtypeStruct(adj_two.shape, kind),
            jax.ShapeDtypeStruct(w_two.shape, kind),
            jax.ShapeDtypeStruct((hidden, tile), jnp.float32),
            jax.ShapeDtypeStruct((plan.table,), jnp.int32),
        ),
        in_specs=[SMEM, VMEM] + [HBM] * 4,
        out_specs=(VMEM,) * 5 + (SMEM,),
        scratch_shapes=[
            pltpu.VMEM((own * tile, hidden), kind),
            pltpu.VMEM((hidden, own * tile), kind),
            pltpu.SMEM((plan.group_tiles,), jnp.int32),
            pltpu.SMEM((plan.slots,), jnp.int32),
            pltpu.SemaphoreType.DMA((3,)),
            pltpu.SemaphoreType.DMA((plan.padded,)),
        ],
        compiler_params=pltpu.CompilerParams(vmem_limit_bytes=34 << 20),
        cost_estimate=pl.CostEstimate(
            flops=2 * plan.entries * tile * tile * hidden, bytes_accessed=20 << 20, transcendentals=0
        ),
        name="prepare",
    )(ints, bias, adj_one, adj_two, w_two, cot)


def call_layer_one(plan, feat_count, table, gathered, bias, adj_one, down):
    blocks = len(gathered)
    tile = adj_one.shape[-1]
    hidden = bias.shape[0]
    features = gathered[0].shape[0] * blocks
    kind = adj_one.dtype
    share = jax.ShapeDtypeStruct((feat_count // 2, 2, features // feat_count, hidden), jnp.float32)
    return pl.pallas_call(
        functools.partial(layer_one_kernel, plan, blocks),
        out_shape=(share, share, jax.ShapeDtypeStruct(down.shape, kind)),
        in_specs=[SMEM] + [VMEM] * (blocks + 3),
        out_specs=(VMEM,) * 3,
        scratch_shapes=[
            pltpu.VMEM((hidden, 2 * features), kind),
            pltpu.VMEM((2 * features, hidden), jnp.float32),
            pltpu.VMEM((2, 2 * features, BATCH * tile), kind),
            pltpu.VMEM((2, hidden, BATCH * tile), kind),
        ],
        compiler_params=pltpu.CompilerParams(vmem_limit_bytes=12 << 20),
        cost_estimate=pl.CostEstimate(
            flops=2 * plan.slots * tile * 2 * features * hidden * 3,
            bytes_accessed=20 << 20,
            transcendentals=plan.slots * tile * hidden,
        ),
        name="layer_one",
    )(table, *gathered, bias, adj_one, down)


def call_layer_two(plan, table, h_tiles, adj_two, w_two):
    own, fan, tile, _ = adj_two.shape
    hidden = w_two.shape[-1]
    kind = h_tiles.dtype
    return pl.pallas_call(
        functools.partial(layer_two_kernel, plan),
        out_shape=jax.ShapeDtypeStruct((own, tile, hidden), kind),
        in_specs=[SMEM, VMEM, VMEM, VMEM],
        out_specs=HBM,
        scratch_shapes=[
            pltpu.VMEM((own, hidden, tile), kind),
            pltpu.VMEM((own, tile, hidden), kind),
            pltpu.SemaphoreType.DMA((own,)),
        ],
        compiler_params=pltpu.CompilerParams(vmem_limit_bytes=12 << 20),
        cost_estimate=pl.CostEstimate(
            flops=2 * plan.entries * tile * tile * hidden, bytes_accessed=8 << 20, transcendentals=0
        ),
        name="layer_two",
    )(table, h_tiles, adj_two, w_two)


def body(
    x_feat,
    place,
    adj_one,
    cols_one,
    count_one,
    w_one,
    bias_one,
    adj_two,
    cols_two,
    count_two,
    w_two,
    cotangent,
):
    x_local = x_feat[0]
    feat_dev = x_local.shape[0]
    tile = adj_one.shape[-1]
    own, fan_two = adj_two.shape[1:3]
    hidden = w_two.shape[-1]
    feat_count = lax.axis_size("feat")
    plan = Plan(place.shape[1], adj_one.shape[2], own, fan_two, place.shape[1] + 2 * hidden // tile)

    nothing = jnp.zeros((feat_dev, tile), x_local.dtype)
    packed = jnp.concatenate([x_local, w_one[0], w_one[1], nothing], axis=1)
    near = [packed] + [exchange(packed, "feat", m) for m in range(2, feat_count, 2)]
    far = [exchange(packed, "feat", 1)]

    me = lax.axis_index("feat").astype(jnp.int32).reshape(1)
    ints = jnp.concatenate(
        [me]
        + [a.reshape(-1) for a in (place, cols_two, count_two, cols_one, count_one)]
    )
    down, adj_near, adj_far, weights, bias, table = call_prepare(
        plan, ints, bias_one.astype(jnp.float32).reshape(1, hidden), adj_one[0], adj_two[0], w_two, cotangent[0]
    )
    near[1:], down = lax.optimization_barrier((near[1:], down))
    far += [exchange(block, "feat", 1) for block in near[1:]]
    gathered = [block for pair in zip(near, far) for block in pair]
    merge = max(1, 16 // feat_dev)
    if merge > 1:
        gathered = [
            jnp.concatenate(gathered[i : i + merge], axis=0) for i in range(0, feat_count, merge)
        ]
    even, odd, h_tiles = call_layer_one(plan, feat_count, table, gathered, bias, adj_near, down)
    layer_out = call_layer_two(plan, table, h_tiles, adj_far, weights)

    even = even + exchange(odd, "feat", 1)
    grad = even[0]
    for received in [exchange(even[j], "feat", 2 * j) for j in range(1, feat_count // 2)]:
        grad = grad + received
    level = [grad] + [exchange(grad, "grp", m) for m in range(1, lax.axis_size("grp"))]
    while len(level) > 1:
        level = [level[i] + level[i + 1] for i in range(0, len(level), 2)]
    return (layer_out.reshape(1, own * tile, hidden), level[0])


def solution(mesh):
    in_specs = (
        P("grp", "feat", None),
        P("grp", None),
        P("grp", None, None, None, None),
        P("grp", None, None),
        P("grp", None),
        P(None, "feat", None),
        P(),
        P("grp", "feat", None, None, None),
        P("grp", "feat", None),
        P("grp", "feat"),
        P(),
        P("grp", "feat", None),
    )
    out_specs = (P("grp", "feat", None), P(None, "feat", None))
    return jax.shard_map(body, mesh=mesh, in_specs=in_specs, out_specs=out_specs, check_vma=False)
```

```python
import functools

import jax
import jax.numpy as jnp
from jax import lax
from jax.experimental import pallas as pl
from jax.experimental.pallas import tpu as pltpu
from jax.sharding import PartitionSpec as P

BATCH = 4
HEAD = 8
NT = (((1,), (1,)), ((), ()))
TN = (((0,), (0,)), ((), ()))
VMEM = pl.BlockSpec(memory_space=pltpu.VMEM)
SMEM = pl.BlockSpec(memory_space=pltpu.SMEM)
HBM = pl.BlockSpec(memory_space=pltpu.HBM)


def dot(a, b, dims=(((1,), (0,)), ((), ()))):
    return lax.dot_general(a, b, dims, preferred_element_type=jnp.float32)


def exchange(array, axis, mask):
    size = lax.axis_size(axis)
    return lax.ppermute(array, axis, [(i, i ^ mask) for i in range(size)])


class Plan:
    def __init__(self, group_tiles, fan_one, own, fan_two):
        self.group_tiles, self.fan_one, self.own, self.fan_two = group_tiles, fan_one, own, fan_two
        self.entries = own * fan_two
        self.dense = self.entries == group_tiles
        self.slots = group_tiles if self.dense else self.entries + own
        self.steps = -(-self.slots // BATCH)
        self.padded = self.steps * BATCH
        self.tile_at = HEAD
        self.slot_at = self.tile_at + self.padded + BATCH
        self.column_at = self.slot_at + self.padded + BATCH
        self.entry_at = self.column_at + (self.padded + BATCH) * fan_one
        self.table = self.entry_at + self.entries


def prepare_kernel(
    plan, place_ref, cols_two_ref, count_two_ref, cols_one_ref, count_one_ref, bias_ref,
    adj_one_ref, adj_two_ref, w_ref, cot_ref,
    d_ref, adj_one, adj_two, w_two, bias, table,
    cot, back, place, cols_two, count_two, cols_one, count_one, inverse, active, sems, adj_sems,
):
    own, fan, fan_one = plan.own, plan.fan_two, plan.fan_one
    tile = adj_two.shape[-1]
    hidden = w_two.shape[-1]
    first = lax.axis_index("feat") * own
    own_slot = first if plan.dense else plan.entries

    pairs = (
        (place_ref, place), (cols_two_ref, cols_two), (count_two_ref, count_two),
        (cols_one_ref, cols_one), (count_one_ref, count_one),
        (w_ref, w_two), (cot_ref, cot), (adj_two_ref, adj_two),
    )
    copies = [pltpu.make_async_copy(source, to, sems.at[i]) for i, (source, to) in enumerate(pairs)]
    for copy in copies:
        copy.start()
    for copy in copies[:5]:
        copy.wait()

    def adj_copy(i):
        t = table[plan.tile_at + i]
        return pltpu.make_async_copy(adj_one_ref.at[t], adj_one.at[i], adj_sems.at[i])

    @pl.loop(0, plan.group_tiles, unroll=8)
    def _(t):
        inverse[place[0, t]] = t

    @pl.loop(0, own)
    def _(p):
        count = count_two[0, p]
        for k in range(fan):
            e = p * fan + k
            slot = cols_two[p, k] if plan.dense else e
            live = k < count
            table[plan.entry_at + e] = jnp.where(live, slot, own_slot)
            if plan.dense:
                mine = jnp.logical_and(slot >= own_slot, slot < own_slot + own)
                live = jnp.logical_or(live, mine)
            active[slot] = live.astype(jnp.int32)
        if not plan.dense:
            active[plan.entries + p] = 1

    def visit(s, n):
        if plan.dense:
            placed = s
        else:
            e = jnp.minimum(s, plan.entries - 1)
            named = cols_two[lax.div(e, fan), lax.rem(e, fan)]
            placed = jnp.where(s < plan.entries, named, first + s - plan.entries)
        table[plan.tile_at + n] = inverse[placed]
        table[plan.slot_at + n] = s
        return n + active[s]

    n = lax.fori_loop(0, plan.slots, visit, jnp.int32(0), unroll=8)
    steps = lax.div(n + BATCH - 1, BATCH)
    table[0] = steps
    table[1] = own_slot

    @pl.loop(n, plan.padded + BATCH)
    def _(i):
        table[plan.tile_at + i] = 0
        table[plan.slot_at + i] = plan.slots + lax.rem(i, BATCH)

    @pl.loop(0, steps + 1)
    def _(step):
        for b in range(BATCH):
            i = step * BATCH + b
            t = table[plan.tile_at + i]
            for k in range(fan_one):
                table[plan.column_at + i * fan_one + k] = cols_one[k, t]

    @pl.loop(0, steps)
    def _(step):
        for b in range(BATCH):
            adj_copy(step * BATCH + b).start()

    for b in range(BATCH):
        d_ref[plan.slots + b] = jnp.zeros((hidden, tile), d_ref.dtype)
    if not plan.dense:
        for p in range(own):
            d_ref[plan.entries + p] = jnp.zeros((hidden, tile), d_ref.dtype)
    bias[...] = jnp.broadcast_to(0.5 * bias_ref[...], (tile, hidden)).T

    copies[5].wait()
    copies[6].wait()
    back[...] = dot(w_two[1], cot[...], NT).astype(back.dtype)
    copies[7].wait()

    @pl.loop(0, own)
    def _(p):
        @pl.loop(count_two[0, p], fan)
        def _(k):
            adj_two[p, k] = jnp.zeros((tile, tile), adj_two.dtype)

    for p in range(own):
        tiles = jnp.concatenate([adj_two[p, k] for k in range(fan)], axis=1)
        term = dot(back[:, p * tile : (p + 1) * tile], tiles).astype(d_ref.dtype)
        for k in range(fan):
            e = p * fan + k
            slot = cols_two[p, k] if plan.dense else e
            d_ref[slot] = term[:, k * tile : (k + 1) * tile]

    self_rows = dot(w_two[0], cot[...], NT)
    for p in range(own):
        mine = self_rows[:, p * tile : (p + 1) * tile] + d_ref[own_slot + p].astype(jnp.float32)
        d_ref[own_slot + p] = mine.astype(d_ref.dtype)

    @pl.loop(0, steps)
    def _(step):
        for b in range(BATCH):
            i = step * BATCH + b
            adj_copy(i).wait()

            @pl.loop(count_one[0, table[plan.tile_at + i]], fan_one)
            def _(k):
                adj_one[i, k] = jnp.zeros((tile, tile), adj_one.dtype)


def layer_one_kernel(plan, blocks, table, *refs):
    x_refs = refs[:blocks]
    bias, adj_one, d_ref, even_ref, odd_ref, h_ref, weight, total, both, downs = refs[blocks:]
    fan = plan.fan_one
    tile = adj_one.shape[-1]
    hidden = bias.shape[0]
    features = x_refs[0].shape[0] * blocks
    steps = table[0]

    def x_tile(t):
        at = pl.ds(pl.multiple_of(t * tile, tile), tile)
        return jnp.concatenate([x[:, at] for x in x_refs], axis=0)

    def lanes(b):
        return slice(b * tile, (b + 1) * tile)

    def aggregate(step):
        at = lax.rem(step, 2)
        for b in range(BATCH):
            i = step * BATCH + b
            j = jnp.minimum(i, plan.padded - 1)
            x_all = [x_tile(table[plan.column_at + i * fan + k]) for k in range(fan)]
            tiles = [adj_one[j, k] for k in range(fan)]
            agg = dot(jnp.concatenate(x_all, axis=1), jnp.concatenate(tiles, axis=1), NT)
            both[at, :features, lanes(b)] = x_tile(table[plan.tile_at + i])
            both[at, features:, lanes(b)] = agg.astype(both.dtype)

    def activate(step):
        at = lax.rem(step, 2)
        for b in range(0, BATCH, 2):
            z = dot(weight[...], both[at, :, b * tile : (b + 2) * tile])
            for c in range(2):
                u = z[:, lanes(c)] + bias[...]
                t = jnp.tanh(u)
                h = u * (1.0 + t)
                slope = (1.0 + t) + h * (1.0 - t)
                slot = table[plan.slot_at + step * BATCH + b + c]
                h_ref[slot] = h.astype(h_ref.dtype)
                down = d_ref[slot].astype(jnp.float32) * slope
                downs[at, :, lanes(b + c)] = down.astype(downs.dtype)

    def contract(step):
        at = lax.rem(step + 2, 2)
        total[...] += dot(both[at], downs[at], NT)

    for part in range(2):
        at = pl.ds(plan.group_tiles * tile + part * hidden, hidden)
        w = jnp.concatenate([x[:, at] for x in x_refs], axis=0)
        weight[:, part * features : (part + 1) * features] = (0.5 * w.astype(jnp.float32)).T.astype(weight.dtype)
    total[...] = jnp.zeros_like(total)
    both[1] = jnp.zeros(both.shape[1:], both.dtype)
    downs[1] = jnp.zeros(downs.shape[1:], downs.dtype)
    aggregate(0)

    @pl.loop(0, steps)
    def _(step):
        contract(step - 1)
        activate(step)
        aggregate(step + 1)

    contract(steps - 1)
    half = even_ref.shape[0]
    share = features // (2 * half)
    for m in range(2 * half):
        out = even_ref if m % 2 == 0 else odd_ref
        for part in range(2):
            at = part * features + m * share
            out[m // 2, part] = 0.5 * total[at : at + share]


def layer_two_kernel(plan, table, h_ref, adj_two, w_ref, out_ref, agg, out, sems):
    own, fan = plan.own, plan.fan_two
    tile = adj_two.shape[-1]
    own_slot = table[1]
    for p in range(own):
        h_all = [h_ref[table[plan.entry_at + p * fan + k]] for k in range(fan)]
        tiles = [adj_two[p, k] for k in range(fan)]
        rows = dot(jnp.concatenate(h_all, axis=1), jnp.concatenate(tiles, axis=1), NT)
        agg[p] = rows.astype(agg.dtype)
    copies = []
    for p in range(own):
        rows = dot(h_ref[own_slot + p], w_ref[0], TN) + dot(agg[p], w_ref[1], TN)
        out[p] = rows.astype(out.dtype)
        copies.append(pltpu.make_async_copy(out.at[p], out_ref.at[p], sems.at[p]))
        copies[-1].start()
    for copy in copies:
        copy.wait()


def call_prepare(plan, ints, bias, adj_one, adj_two, w_two, cot):
    adj_one, adj_two, w_two, cot, *ints = [
        pltpu.with_memory_space_constraint(a, pltpu.HBM) for a in (adj_one, adj_two, w_two, cot, *ints)
    ]
    own, fan, tile, _ = adj_two.shape
    hidden = w_two.shape[-1]
    kind = adj_one.dtype
    return pl.pallas_call(
        functools.partial(prepare_kernel, plan),
        out_shape=(
            jax.ShapeDtypeStruct((plan.slots + BATCH, hidden, tile), kind),
            jax.ShapeDtypeStruct((plan.padded, plan.fan_one, tile, tile), kind),
            jax.ShapeDtypeStruct(adj_two.shape, kind),
            jax.ShapeDtypeStruct(w_two.shape, kind),
            jax.ShapeDtypeStruct((hidden, tile), jnp.float32),
            jax.ShapeDtypeStruct((plan.table,), jnp.int32),
        ),
        in_specs=[HBM] * 5 + [VMEM] + [HBM] * 4,
        out_specs=(VMEM,) * 5 + (SMEM,),
        scratch_shapes=[
            pltpu.VMEM((own * tile, hidden), kind),
            pltpu.VMEM((hidden, own * tile), kind),
            *[pltpu.SMEM(a.shape, jnp.int32) for a in ints],
            pltpu.SMEM((plan.group_tiles,), jnp.int32),
            pltpu.SMEM((plan.slots,), jnp.int32),
            pltpu.SemaphoreType.DMA((8,)),
            pltpu.SemaphoreType.DMA((plan.padded,)),
        ],
        compiler_params=pltpu.CompilerParams(vmem_limit_bytes=34 << 20),
        cost_estimate=pl.CostEstimate(
            flops=2 * plan.entries * tile * tile * hidden, bytes_accessed=20 << 20, transcendentals=0
        ),
        name="prepare",
    )(*ints, bias, adj_one, adj_two, w_two, cot)


def call_layer_one(plan, feat_count, table, gathered, bias, adj_one, down):
    blocks = len(gathered)
    tile = adj_one.shape[-1]
    hidden = bias.shape[0]
    features = gathered[0].shape[0] * blocks
    kind = adj_one.dtype
    share = jax.ShapeDtypeStruct((feat_count // 2, 2, features // feat_count, hidden), jnp.float32)
    return pl.pallas_call(
        functools.partial(layer_one_kernel, plan, blocks),
        out_shape=(share, share, jax.ShapeDtypeStruct(down.shape, kind)),
        in_specs=[SMEM] + [VMEM] * (blocks + 3),
        out_specs=(VMEM,) * 3,
        scratch_shapes=[
            pltpu.VMEM((hidden, 2 * features), kind),
            pltpu.VMEM((2 * features, hidden), jnp.float32),
            pltpu.VMEM((2, 2 * features, BATCH * tile), kind),
            pltpu.VMEM((2, hidden, BATCH * tile), kind),
        ],
        compiler_params=pltpu.CompilerParams(vmem_limit_bytes=12 << 20),
        cost_estimate=pl.CostEstimate(
            flops=2 * plan.slots * tile * 2 * features * hidden * 3,
            bytes_accessed=20 << 20,
            transcendentals=plan.slots * tile * hidden,
        ),
        name="layer_one",
    )(table, *gathered, bias, adj_one, down)


def call_layer_two(plan, table, h_tiles, adj_two, w_two):
    own, fan, tile, _ = adj_two.shape
    hidden = w_two.shape[-1]
    kind = h_tiles.dtype
    return pl.pallas_call(
        functools.partial(layer_two_kernel, plan),
        out_shape=jax.ShapeDtypeStruct((own, tile, hidden), kind),
        in_specs=[SMEM, VMEM, VMEM, VMEM],
        out_specs=HBM,
        scratch_shapes=[
            pltpu.VMEM((own, hidden, tile), kind),
            pltpu.VMEM((own, tile, hidden), kind),
            pltpu.SemaphoreType.DMA((own,)),
        ],
        compiler_params=pltpu.CompilerParams(vmem_limit_bytes=12 << 20),
        cost_estimate=pl.CostEstimate(
            flops=2 * plan.entries * tile * tile * hidden, bytes_accessed=8 << 20, transcendentals=0
        ),
        name="layer_two",
    )(table, h_tiles, adj_two, w_two)


def body(
    x_feat,
    place,
    adj_one,
    cols_one,
    count_one,
    w_one,
    bias_one,
    adj_two,
    cols_two,
    count_two,
    w_two,
    cotangent,
):
    x_local = x_feat[0]
    feat_dev = x_local.shape[0]
    tile = adj_one.shape[-1]
    own, fan_two = adj_two.shape[1:3]
    hidden = w_two.shape[-1]
    feat_count = lax.axis_size("feat")
    plan = Plan(place.shape[1], adj_one.shape[2], own, fan_two)

    packed = jnp.concatenate([x_local, w_one[0], w_one[1]], axis=1)
    near = [packed] + [exchange(packed, "feat", m) for m in range(2, feat_count, 2)]
    far = [exchange(packed, "feat", 1)]

    ints = (place, cols_two[0], count_two, cols_one[0].T, count_one)
    down, adj_near, adj_far, weights, bias, table = call_prepare(
        plan, ints, bias_one.astype(jnp.float32).reshape(1, hidden), adj_one[0], adj_two[0], w_two, cotangent[0]
    )
    near[1:], down = lax.optimization_barrier((near[1:], down))
    far += [exchange(block, "feat", 1) for block in near[1:]]
    gathered = [block for pair in zip(near, far) for block in pair]
    merge = max(1, 16 // feat_dev)
    if merge > 1:
        gathered = [
            jnp.concatenate(gathered[i : i + merge], axis=0) for i in range(0, feat_count, merge)
        ]
    even, odd, h_tiles = call_layer_one(plan, feat_count, table, gathered, bias, adj_near, down)
    layer_out = call_layer_two(plan, table, h_tiles, adj_far, weights)

    even = even + exchange(odd, "feat", 1)
    grad = even[0]
    for received in [exchange(even[j], "feat", 2 * j) for j in range(1, feat_count // 2)]:
        grad = grad + received
    level = [grad] + [exchange(grad, "grp", m) for m in range(1, lax.axis_size("grp"))]
    while len(level) > 1:
        level = [level[i] + level[i + 1] for i in range(0, len(level), 2)]
    return (layer_out.reshape(1, own * tile, hidden), level[0])


def solution(mesh):
    in_specs = (
        P("grp", "feat", None),
        P("grp", None),
        P("grp", None, None, None, None),
        P("grp", None, None),
        P("grp", None),
        P(None, "feat", None),
        P(),
        P("grp", "feat", None, None, None),
        P("grp", "feat", None),
        P("grp", "feat"),
        P(),
        P("grp", "feat", None),
    )
    out_specs = (P("grp", "feat", None), P(None, "feat", None))
    return jax.shard_map(body, mesh=mesh, in_specs=in_specs, out_specs=out_specs, check_vma=False)
```

```python
import functools

import jax
import jax.numpy as jnp
from jax import lax
from jax.experimental import pallas as pl
from jax.experimental.pallas import tpu as pltpu
from jax.sharding import PartitionSpec as P

BATCH = 4
HEAD = 8
NT = (((1,), (1,)), ((), ()))
TN = (((0,), (0,)), ((), ()))
VMEM = pl.BlockSpec(memory_space=pltpu.VMEM)
SMEM = pl.BlockSpec(memory_space=pltpu.SMEM)
HBM = pl.BlockSpec(memory_space=pltpu.HBM)


def dot(a, b, dims=(((1,), (0,)), ((), ()))):
    return lax.dot_general(a, b, dims, preferred_element_type=jnp.float32)


def exchange(array, axis, mask):
    size = lax.axis_size(axis)
    return lax.ppermute(array, axis, [(i, i ^ mask) for i in range(size)])


class Plan:
    def __init__(self, group_tiles, fan_one, own, fan_two):
        self.group_tiles, self.fan_one, self.own, self.fan_two = group_tiles, fan_one, own, fan_two
        self.entries = own * fan_two
        self.dense = self.entries == group_tiles
        self.slots = group_tiles if self.dense else self.entries + own
        self.few = fan_one // 2
        self.steps = -(-self.slots // BATCH) + 1
        self.padded = self.steps * BATCH
        self.tile_at = HEAD
        self.slot_at = self.tile_at + self.padded + BATCH
        self.column_at = self.slot_at + self.padded + BATCH
        self.entry_at = self.column_at + (self.padded + BATCH) * fan_one
        self.table = self.entry_at + self.entries


def prepare_kernel(
    plan, place_ref, cols_two_ref, count_two_ref, cols_one_ref, count_one_ref, bias_ref,
    adj_one_ref, adj_two_ref, w_ref, cot_ref,
    d_ref, adj_one, adj_two, w_two, bias, table,
    cot, back, place, cols_two, count_two, cols_one, count_one, inverse, active, sems, adj_sems,
):
    own, fan, fan_one = plan.own, plan.fan_two, plan.fan_one
    tile = adj_two.shape[-1]
    hidden = w_two.shape[-1]
    first = lax.axis_index("feat") * own
    own_slot = first if plan.dense else plan.entries

    pairs = (
        (place_ref, place), (cols_two_ref, cols_two), (count_two_ref, count_two),
        (cols_one_ref, cols_one), (count_one_ref, count_one),
        (w_ref, w_two), (cot_ref, cot), (adj_two_ref, adj_two),
    )
    copies = [pltpu.make_async_copy(source, to, sems.at[i]) for i, (source, to) in enumerate(pairs)]
    for copy in copies:
        copy.start()
    for copy in copies[:5]:
        copy.wait()

    def adj_copy(i):
        t = table[plan.tile_at + i]
        return pltpu.make_async_copy(adj_one_ref.at[t], adj_one.at[i], adj_sems.at[i])

    @pl.loop(0, plan.group_tiles, unroll=8)
    def _(t):
        inverse[place[0, t]] = t

    @pl.loop(0, own)
    def _(p):
        count = count_two[0, p]
        for k in range(fan):
            e = p * fan + k
            slot = cols_two[p, k] if plan.dense else e
            live = k < count
            table[plan.entry_at + e] = jnp.where(live, slot, own_slot)
            if plan.dense:
                mine = jnp.logical_and(slot >= own_slot, slot < own_slot + own)
                live = jnp.logical_or(live, mine)
            active[slot] = live.astype(jnp.int32)
        if not plan.dense:
            active[plan.entries + p] = 1

    def pad(start, end):
        @pl.loop(start, end)
        def _(i):
            table[plan.tile_at + i] = 0
            table[plan.slot_at + i] = plan.slots + lax.rem(i, BATCH)

    def whole_steps(n):
        return lax.div(n + BATCH - 1, BATCH)

    def visit(few, s, n):
        if plan.dense:
            placed = s
        else:
            e = jnp.minimum(s, plan.entries - 1)
            named = cols_two[lax.div(e, fan), lax.rem(e, fan)]
            placed = jnp.where(s < plan.entries, named, first + s - plan.entries)
        t = inverse[placed]
        table[plan.tile_at + n] = t
        table[plan.slot_at + n] = s
        count = count_one[0, t]
        fits = count <= plan.few if few else count > plan.few
        return n + jnp.where(fits, active[s], 0)

    n = lax.fori_loop(0, plan.slots, functools.partial(visit, True), jnp.int32(0), unroll=8)
    few_steps = whole_steps(n)
    pad(n, few_steps * BATCH)
    n = lax.fori_loop(0, plan.slots, functools.partial(visit, False), few_steps * BATCH, unroll=8)
    steps = whole_steps(n)
    pad(n, plan.padded + BATCH)
    table[0] = steps
    table[1] = own_slot
    table[2] = few_steps

    @pl.loop(0, steps + 1)
    def _(step):
        for b in range(BATCH):
            i = step * BATCH + b
            t = table[plan.tile_at + i]
            for k in range(fan_one):
                table[plan.column_at + i * fan_one + k] = cols_one[k, t]

    @pl.loop(0, steps)
    def _(step):
        for b in range(BATCH):
            adj_copy(step * BATCH + b).start()

    for b in range(BATCH):
        d_ref[plan.slots + b] = jnp.zeros((hidden, tile), d_ref.dtype)
    if not plan.dense:
        for p in range(own):
            d_ref[plan.entries + p] = jnp.zeros((hidden, tile), d_ref.dtype)
    bias[...] = jnp.broadcast_to(0.5 * bias_ref[...], (tile, hidden)).T

    copies[5].wait()
    copies[6].wait()
    back[...] = dot(w_two[1], cot[...], NT).astype(back.dtype)
    copies[7].wait()

    @pl.loop(0, own)
    def _(p):
        @pl.loop(count_two[0, p], fan)
        def _(k):
            adj_two[p, k] = jnp.zeros((tile, tile), adj_two.dtype)

    for p in range(own):
        tiles = jnp.concatenate([adj_two[p, k] for k in range(fan)], axis=1)
        term = dot(back[:, p * tile : (p + 1) * tile], tiles).astype(d_ref.dtype)
        for k in range(fan):
            e = p * fan + k
            slot = cols_two[p, k] if plan.dense else e
            d_ref[slot] = term[:, k * tile : (k + 1) * tile]

    self_rows = dot(w_two[0], cot[...], NT)
    for p in range(own):
        mine = self_rows[:, p * tile : (p + 1) * tile] + d_ref[own_slot + p].astype(jnp.float32)
        d_ref[own_slot + p] = mine.astype(d_ref.dtype)

    @pl.loop(0, steps)
    def _(step):
        for b in range(BATCH):
            i = step * BATCH + b
            adj_copy(i).wait()

            @pl.loop(count_one[0, table[plan.tile_at + i]], fan_one)
            def _(k):
                adj_one[i, k] = jnp.zeros((tile, tile), adj_one.dtype)


def layer_one_kernel(plan, blocks, table, *refs):
    x_refs = refs[:blocks]
    bias, adj_one, d_ref, even_ref, odd_ref, h_ref, weight, total, both, downs = refs[blocks:]
    tile = adj_one.shape[-1]
    hidden = bias.shape[0]
    features = x_refs[0].shape[0] * blocks
    steps = table[0]

    def x_tile(t):
        at = pl.ds(pl.multiple_of(t * tile, tile), tile)
        return jnp.concatenate([x[:, at] for x in x_refs], axis=0)

    def lanes(b):
        return slice(b * tile, (b + 1) * tile)

    def aggregate(step, fan):
        at = lax.rem(step, 2)
        for b in range(BATCH):
            i = step * BATCH + b
            j = jnp.minimum(i, plan.padded - 1)
            x_all = [x_tile(table[plan.column_at + i * plan.fan_one + k]) for k in range(fan)]
            tiles = [adj_one[j, k] for k in range(fan)]
            agg = dot(jnp.concatenate(x_all, axis=1), jnp.concatenate(tiles, axis=1), NT)
            both[at, :features, lanes(b)] = x_tile(table[plan.tile_at + i])
            both[at, features:, lanes(b)] = agg.astype(both.dtype)

    def activate(step):
        at = lax.rem(step, 2)
        for b in range(0, BATCH, 2):
            z = dot(weight[...], both[at, :, b * tile : (b + 2) * tile])
            for c in range(2):
                u = z[:, lanes(c)] + bias[...]
                t = jnp.tanh(u)
                h = u * (1.0 + t)
                slope = (1.0 + t) + h * (1.0 - t)
                slot = table[plan.slot_at + step * BATCH + b + c]
                h_ref[slot] = h.astype(h_ref.dtype)
                down = d_ref[slot].astype(jnp.float32) * slope
                downs[at, :, lanes(b + c)] = down.astype(downs.dtype)

    def contract(step):
        at = lax.rem(step + 2, 2)
        total[...] += dot(both[at], downs[at], NT)

    for part in range(2):
        at = pl.ds(plan.group_tiles * tile + part * hidden, hidden)
        w = jnp.concatenate([x[:, at] for x in x_refs], axis=0)
        weight[:, part * features : (part + 1) * features] = (0.5 * w.astype(jnp.float32)).T.astype(weight.dtype)
    total[...] = jnp.zeros_like(total)
    both[1] = jnp.zeros(both.shape[1:], both.dtype)
    downs[1] = jnp.zeros(downs.shape[1:], downs.dtype)
    aggregate(0, plan.fan_one)
    turn = jnp.maximum(table[2] - 1, 0)

    @pl.loop(0, turn)
    def _(step):
        contract(step - 1)
        activate(step)
        aggregate(step + 1, plan.few)

    @pl.loop(turn, steps)
    def _(step):
        contract(step - 1)
        activate(step)
        aggregate(step + 1, plan.fan_one)

    contract(steps - 1)
    half = even_ref.shape[0]
    share = features // (2 * half)
    for m in range(2 * half):
        out = even_ref if m % 2 == 0 else odd_ref
        for part in range(2):
            at = part * features + m * share
            out[m // 2, part] = 0.5 * total[at : at + share]


def layer_two_kernel(plan, table, h_ref, adj_two, w_ref, out_ref, agg, out, sems):
    own, fan = plan.own, plan.fan_two
    tile = adj_two.shape[-1]
    own_slot = table[1]
    for p in range(own):
        h_all = [h_ref[table[plan.entry_at + p * fan + k]] for k in range(fan)]
        tiles = [adj_two[p, k] for k in range(fan)]
        rows = dot(jnp.concatenate(h_all, axis=1), jnp.concatenate(tiles, axis=1), NT)
        agg[p] = rows.astype(agg.dtype)
    copies = []
    for p in range(own):
        rows = dot(h_ref[own_slot + p], w_ref[0], TN) + dot(agg[p], w_ref[1], TN)
        out[p] = rows.astype(out.dtype)
        copies.append(pltpu.make_async_copy(out.at[p], out_ref.at[p], sems.at[p]))
        copies[-1].start()
    for copy in copies:
        copy.wait()


def call_prepare(plan, ints, bias, adj_one, adj_two, w_two, cot):
    adj_one, adj_two, w_two, cot, *ints = [
        pltpu.with_memory_space_constraint(a, pltpu.HBM) for a in (adj_one, adj_two, w_two, cot, *ints)
    ]
    own, fan, tile, _ = adj_two.shape
    hidden = w_two.shape[-1]
    kind = adj_one.dtype
    return pl.pallas_call(
        functools.partial(prepare_kernel, plan),
        out_shape=(
            jax.ShapeDtypeStruct((plan.slots + BATCH, hidden, tile), kind),
            jax.ShapeDtypeStruct((plan.padded, plan.fan_one, tile, tile), kind),
            jax.ShapeDtypeStruct(adj_two.shape, kind),
            jax.ShapeDtypeStruct(w_two.shape, kind),
            jax.ShapeDtypeStruct((hidden, tile), jnp.float32),
            jax.ShapeDtypeStruct((plan.table,), jnp.int32),
        ),
        in_specs=[HBM] * 5 + [VMEM] + [HBM] * 4,
        out_specs=(VMEM,) * 5 + (SMEM,),
        scratch_shapes=[
            pltpu.VMEM((own * tile, hidden), kind),
            pltpu.VMEM((hidden, own * tile), kind),
            *[pltpu.SMEM(a.shape, jnp.int32) for a in ints],
            pltpu.SMEM((plan.group_tiles,), jnp.int32),
            pltpu.SMEM((plan.slots,), jnp.int32),
            pltpu.SemaphoreType.DMA((8,)),
            pltpu.SemaphoreType.DMA((plan.padded,)),
        ],
        compiler_params=pltpu.CompilerParams(vmem_limit_bytes=34 << 20),
        cost_estimate=pl.CostEstimate(flops=0, bytes_accessed=1 << 16, transcendentals=0),
        name="prepare",
    )(*ints, bias, adj_one, adj_two, w_two, cot)


def call_layer_one(plan, feat_count, table, gathered, bias, adj_one, down):
    blocks = len(gathered)
    tile = adj_one.shape[-1]
    hidden = bias.shape[0]
    features = gathered[0].shape[0] * blocks
    kind = adj_one.dtype
    share = jax.ShapeDtypeStruct((feat_count // 2, 2, features // feat_count, hidden), jnp.float32)
    return pl.pallas_call(
        functools.partial(layer_one_kernel, plan, blocks),
        out_shape=(share, share, jax.ShapeDtypeStruct(down.shape, kind)),
        in_specs=[SMEM] + [VMEM] * (blocks + 3),
        out_specs=(VMEM,) * 3,
        scratch_shapes=[
            pltpu.VMEM((hidden, 2 * features), kind),
            pltpu.VMEM((2 * features, hidden), jnp.float32),
            pltpu.VMEM((2, 2 * features, BATCH * tile), kind),
            pltpu.VMEM((2, hidden, BATCH * tile), kind),
        ],
        compiler_params=pltpu.CompilerParams(vmem_limit_bytes=12 << 20),
        cost_estimate=pl.CostEstimate(
            flops=2 * plan.slots * tile * 2 * features * hidden * 3,
            bytes_accessed=20 << 20,
            transcendentals=plan.slots * tile * hidden,
        ),
        name="layer_one",
    )(table, *gathered, bias, adj_one, down)


def call_layer_two(plan, table, h_tiles, adj_two, w_two):
    own, fan, tile, _ = adj_two.shape
    hidden = w_two.shape[-1]
    kind = h_tiles.dtype
    return pl.pallas_call(
        functools.partial(layer_two_kernel, plan),
        out_shape=jax.ShapeDtypeStruct((own, tile, hidden), kind),
        in_specs=[SMEM, VMEM, VMEM, VMEM],
        out_specs=HBM,
        scratch_shapes=[
            pltpu.VMEM((own, hidden, tile), kind),
            pltpu.VMEM((own, tile, hidden), kind),
            pltpu.SemaphoreType.DMA((own,)),
        ],
        compiler_params=pltpu.CompilerParams(vmem_limit_bytes=12 << 20),
        cost_estimate=pl.CostEstimate(
            flops=2 * plan.entries * tile * tile * hidden, bytes_accessed=8 << 20, transcendentals=0
        ),
        name="layer_two",
    )(table, h_tiles, adj_two, w_two)


def body(
    x_feat,
    place,
    adj_one,
    cols_one,
    count_one,
    w_one,
    bias_one,
    adj_two,
    cols_two,
    count_two,
    w_two,
    cotangent,
):
    x_local = x_feat[0]
    feat_dev = x_local.shape[0]
    tile = adj_one.shape[-1]
    own, fan_two = adj_two.shape[1:3]
    hidden = w_two.shape[-1]
    feat_count = lax.axis_size("feat")
    plan = Plan(place.shape[1], adj_one.shape[2], own, fan_two)

    packed = jnp.concatenate([x_local, w_one[0], w_one[1]], axis=1)
    near = [packed] + [exchange(packed, "feat", m) for m in range(2, feat_count, 2)]
    far = [exchange(packed, "feat", 1)]

    ints = (place, cols_two[0], count_two, cols_one[0].T, count_one)
    down, adj_near, adj_far, weights, bias, table = call_prepare(
        plan, ints, bias_one.astype(jnp.float32).reshape(1, hidden), adj_one[0], adj_two[0], w_two, cotangent[0]
    )
    near[1:-1], down = lax.optimization_barrier((near[1:-1], down))
    far += [exchange(block, "feat", 1) for block in near[1:-1]]
    near[-1], far[1:] = lax.optimization_barrier((near[-1], far[1:]))
    far.append(exchange(near[-1], "feat", 1))
    gathered = [block for pair in zip(near, far) for block in pair]
    merge = max(1, 16 // feat_dev)
    if merge > 1:
        gathered = [
            jnp.concatenate(gathered[i : i + merge], axis=0) for i in range(0, feat_count, merge)
        ]
    even, odd, h_tiles = call_layer_one(plan, feat_count, table, gathered, bias, adj_near, down)
    layer_out = call_layer_two(plan, table, h_tiles, adj_far, weights)

    even = even + exchange(odd, "feat", 1)
    grad = even[0]
    for received in [exchange(even[j], "feat", 2 * j) for j in range(1, feat_count // 2)]:
        grad = grad + received
    level = [grad] + [exchange(grad, "grp", m) for m in range(1, lax.axis_size("grp"))]
    while len(level) > 1:
        level = [level[i] + level[i + 1] for i in range(0, len(level), 2)]
    return (layer_out.reshape(1, own * tile, hidden), level[0])


def solution(mesh):
    in_specs = (
        P("grp", "feat", None),
        P("grp", None),
        P("grp", None, None, None, None),
        P("grp", None, None),
        P("grp", None),
        P(None, "feat", None),
        P(),
        P("grp", "feat", None, None, None),
        P("grp", "feat", None),
        P("grp", "feat"),
        P(),
        P("grp", "feat", None),
    )
    out_specs = (P("grp", "feat", None), P(None, "feat", None))
    return jax.shard_map(body, mesh=mesh, in_specs=in_specs, out_specs=out_specs, check_vma=False)
```

```python
import functools

import jax
import jax.numpy as jnp
from jax import lax
from jax.experimental import pallas as pl
from jax.experimental.pallas import tpu as pltpu
from jax.sharding import PartitionSpec as P

BATCH = 4
HEAD = 8
NT = (((1,), (1,)), ((), ()))
TN = (((0,), (0,)), ((), ()))
VMEM = pl.BlockSpec(memory_space=pltpu.VMEM)
SMEM = pl.BlockSpec(memory_space=pltpu.SMEM)
HBM = pl.BlockSpec(memory_space=pltpu.HBM)


def dot(a, b, dims=(((1,), (0,)), ((), ()))):
    return lax.dot_general(a, b, dims, preferred_element_type=jnp.float32)


def exchange(array, axis, mask):
    size = lax.axis_size(axis)
    return lax.ppermute(array, axis, [(i, i ^ mask) for i in range(size)])


class Plan:
    def __init__(self, group_tiles, fan_one, own, fan_two):
        self.group_tiles, self.fan_one, self.own, self.fan_two = group_tiles, fan_one, own, fan_two
        self.entries = own * fan_two
        self.dense = self.entries == group_tiles
        self.slots = group_tiles if self.dense else self.entries + own
        self.few = fan_one // 2
        self.steps = -(-self.slots // BATCH)
        self.padded = self.steps * BATCH
        self.tile_at = HEAD
        self.slot_at = self.tile_at + self.padded + BATCH
        self.column_at = self.slot_at + self.padded + BATCH
        self.entry_at = self.column_at + (self.padded + BATCH) * fan_one
        self.table = self.entry_at + self.entries


def prepare_kernel(
    plan, place_ref, cols_two_ref, count_two_ref, cols_one_ref, count_one_ref, bias_ref,
    adj_one_ref, adj_two_ref, w_ref, cot_ref,
    d_ref, adj_one, adj_two, w_two, bias, table,
    cot, back, place, cols_two, count_two, cols_one, count_one, inverse, active, sems, adj_sems,
):
    own, fan, fan_one = plan.own, plan.fan_two, plan.fan_one
    tile = adj_two.shape[-1]
    hidden = w_two.shape[-1]
    first = lax.axis_index("feat") * own
    own_slot = first if plan.dense else plan.entries

    pairs = (
        (place_ref, place), (cols_two_ref, cols_two), (count_two_ref, count_two),
        (cols_one_ref, cols_one), (count_one_ref, count_one),
        (w_ref, w_two), (cot_ref, cot), (adj_two_ref, adj_two),
    )
    copies = [pltpu.make_async_copy(source, to, sems.at[i]) for i, (source, to) in enumerate(pairs)]
    for copy in copies:
        copy.start()
    for copy in copies[:5]:
        copy.wait()

    def adj_copy(i):
        t = table[plan.tile_at + i]
        return pltpu.make_async_copy(adj_one_ref.at[t], adj_one.at[i], adj_sems.at[i])

    @pl.loop(0, plan.group_tiles, unroll=8)
    def _(t):
        inverse[place[0, t]] = t

    @pl.loop(0, own)
    def _(p):
        count = count_two[0, p]
        for k in range(fan):
            e = p * fan + k
            slot = cols_two[p, k] if plan.dense else e
            live = k < count
            table[plan.entry_at + e] = jnp.where(live, slot, own_slot)
            if plan.dense:
                mine = jnp.logical_and(slot >= own_slot, slot < own_slot + own)
                live = jnp.logical_or(live, mine)
            active[slot] = live.astype(jnp.int32)
        if not plan.dense:
            active[plan.entries + p] = 1

    def visit(few, s, n):
        if plan.dense:
            placed = s
        else:
            e = jnp.minimum(s, plan.entries - 1)
            named = cols_two[lax.div(e, fan), lax.rem(e, fan)]
            placed = jnp.where(s < plan.entries, named, first + s - plan.entries)
        t = inverse[placed]
        table[plan.tile_at + n] = t
        table[plan.slot_at + n] = s
        count = count_one[0, t]
        fits = count <= plan.few if few else count > plan.few
        return n + jnp.where(fits, active[s], 0)

    n = lax.fori_loop(0, plan.slots, functools.partial(visit, True), jnp.int32(0), unroll=8)
    few_steps = lax.div(n, BATCH)
    n = lax.fori_loop(0, plan.slots, functools.partial(visit, False), n, unroll=8)
    steps = lax.div(n + BATCH - 1, BATCH)

    @pl.loop(n, plan.padded + BATCH)
    def _(i):
        table[plan.tile_at + i] = 0
        table[plan.slot_at + i] = plan.slots + lax.rem(i, BATCH)

    table[0] = steps
    table[1] = own_slot
    table[2] = few_steps

    @pl.loop(0, steps + 1)
    def _(step):
        for b in range(BATCH):
            i = step * BATCH + b
            t = table[plan.tile_at + i]
            for k in range(fan_one):
                table[plan.column_at + i * fan_one + k] = cols_one[k, t]

    @pl.loop(0, steps)
    def _(step):
        for b in range(BATCH):
            adj_copy(step * BATCH + b).start()

    for b in range(BATCH):
        d_ref[plan.slots + b] = jnp.zeros((hidden, tile), d_ref.dtype)
    if not plan.dense:
        for p in range(own):
            d_ref[plan.entries + p] = jnp.zeros((hidden, tile), d_ref.dtype)
    bias[...] = jnp.broadcast_to(0.5 * bias_ref[...], (tile, hidden)).T

    copies[5].wait()
    copies[6].wait()
    back[...] = dot(w_two[1], cot[...], NT).astype(back.dtype)
    copies[7].wait()

    @pl.loop(0, own)
    def _(p):
        @pl.loop(count_two[0, p], fan)
        def _(k):
            adj_two[p, k] = jnp.zeros((tile, tile), adj_two.dtype)

    for p in range(own):
        tiles = jnp.concatenate([adj_two[p, k] for k in range(fan)], axis=1)
        term = dot(back[:, p * tile : (p + 1) * tile], tiles).astype(d_ref.dtype)
        for k in range(fan):
            e = p * fan + k
            slot = cols_two[p, k] if plan.dense else e
            d_ref[slot] = term[:, k * tile : (k + 1) * tile]

    self_rows = dot(w_two[0], cot[...], NT)
    for p in range(own):
        mine = self_rows[:, p * tile : (p + 1) * tile] + d_ref[own_slot + p].astype(jnp.float32)
        d_ref[own_slot + p] = mine.astype(d_ref.dtype)

    @pl.loop(0, steps)
    def _(step):
        for b in range(BATCH):
            i = step * BATCH + b
            adj_copy(i).wait()

            @pl.loop(count_one[0, table[plan.tile_at + i]], fan_one)
            def _(k):
                adj_one[i, k] = jnp.zeros((tile, tile), adj_one.dtype)


def layer_one_kernel(plan, blocks, table, *refs):
    x_refs = refs[:blocks]
    bias, adj_one, d_ref, even_ref, odd_ref, h_ref, weight, total, both, downs = refs[blocks:]
    tile = adj_one.shape[-1]
    hidden = bias.shape[0]
    features = x_refs[0].shape[0] * blocks
    steps = table[0]

    def x_tile(t):
        at = pl.ds(pl.multiple_of(t * tile, tile), tile)
        return jnp.concatenate([x[:, at] for x in x_refs], axis=0)

    def lanes(b):
        return slice(b * tile, (b + 1) * tile)

    def aggregate(step, fan):
        at = lax.rem(step, 2)
        for b in range(BATCH):
            i = step * BATCH + b
            j = jnp.minimum(i, plan.padded - 1)
            x_all = [x_tile(table[plan.column_at + i * plan.fan_one + k]) for k in range(fan)]
            tiles = [adj_one[j, k] for k in range(fan)]
            agg = dot(jnp.concatenate(x_all, axis=1), jnp.concatenate(tiles, axis=1), NT)
            both[at, :features, lanes(b)] = x_tile(table[plan.tile_at + i])
            both[at, features:, lanes(b)] = agg.astype(both.dtype)

    def activate(step):
        at = lax.rem(step, 2)
        for b in range(0, BATCH, 2):
            z = dot(weight[...], both[at, :, b * tile : (b + 2) * tile])
            for c in range(2):
                u = z[:, lanes(c)] + bias[...]
                t = jnp.tanh(u)
                h = u * (1.0 + t)
                slope = (1.0 + t) + h * (1.0 - t)
                slot = table[plan.slot_at + step * BATCH + b + c]
                h_ref[slot] = h.astype(h_ref.dtype)
                down = d_ref[slot].astype(jnp.float32) * slope
                downs[at, :, lanes(b + c)] = down.astype(downs.dtype)

    def contract(step):
        at = lax.rem(step + 2, 2)
        total[...] += dot(both[at], downs[at], NT)

    for part in range(2):
        at = pl.ds(plan.group_tiles * tile + part * hidden, hidden)
        w = jnp.concatenate([x[:, at] for x in x_refs], axis=0)
        weight[:, part * features : (part + 1) * features] = (0.5 * w.astype(jnp.float32)).T.astype(weight.dtype)
    total[...] = jnp.zeros_like(total)
    both[1] = jnp.zeros(both.shape[1:], both.dtype)
    downs[1] = jnp.zeros(downs.shape[1:], downs.dtype)
    aggregate(0, plan.fan_one)
    turn = jnp.maximum(table[2] - 1, 0)

    @pl.loop(0, turn)
    def _(step):
        contract(step - 1)
        activate(step)
        aggregate(step + 1, plan.few)

    @pl.loop(turn, steps)
    def _(step):
        contract(step - 1)
        activate(step)
        aggregate(step + 1, plan.fan_one)

    contract(steps - 1)
    half = even_ref.shape[0]
    share = features // (2 * half)
    for m in range(2 * half):
        out = even_ref if m % 2 == 0 else odd_ref
        for part in range(2):
            at = part * features + m * share
            out[m // 2, part] = 0.5 * total[at : at + share]


def layer_two_kernel(plan, table, h_ref, adj_two, w_ref, out_ref, agg, out, sems):
    own, fan = plan.own, plan.fan_two
    tile = adj_two.shape[-1]
    own_slot = table[1]
    for p in range(own):
        h_all = [h_ref[table[plan.entry_at + p * fan + k]] for k in range(fan)]
        tiles = [adj_two[p, k] for k in range(fan)]
        rows = dot(jnp.concatenate(h_all, axis=1), jnp.concatenate(tiles, axis=1), NT)
        agg[p] = rows.astype(agg.dtype)
    copies = []
    for p in range(own):
        rows = dot(h_ref[own_slot + p], w_ref[0], TN) + dot(agg[p], w_ref[1], TN)
        out[p] = rows.astype(out.dtype)
        copies.append(pltpu.make_async_copy(out.at[p], out_ref.at[p], sems.at[p]))
        copies[-1].start()
    for copy in copies:
        copy.wait()


def call_prepare(plan, ints, bias, adj_one, adj_two, w_two, cot):
    adj_one, adj_two, w_two, cot, *ints = [
        pltpu.with_memory_space_constraint(a, pltpu.HBM) for a in (adj_one, adj_two, w_two, cot, *ints)
    ]
    own, fan, tile, _ = adj_two.shape
    hidden = w_two.shape[-1]
    kind = adj_one.dtype
    return pl.pallas_call(
        functools.partial(prepare_kernel, plan),
        out_shape=(
            jax.ShapeDtypeStruct((plan.slots + BATCH, hidden, tile), kind),
            jax.ShapeDtypeStruct((plan.padded, plan.fan_one, tile, tile), kind),
            jax.ShapeDtypeStruct(adj_two.shape, kind),
            jax.ShapeDtypeStruct(w_two.shape, kind),
            jax.ShapeDtypeStruct((hidden, tile), jnp.float32),
            jax.ShapeDtypeStruct((plan.table,), jnp.int32),
        ),
        in_specs=[HBM] * 5 + [VMEM] + [HBM] * 4,
        out_specs=(VMEM,) * 5 + (SMEM,),
        scratch_shapes=[
            pltpu.VMEM((own * tile, hidden), kind),
            pltpu.VMEM((hidden, own * tile), kind),
            *[pltpu.SMEM(a.shape, jnp.int32) for a in ints],
            pltpu.SMEM((plan.group_tiles,), jnp.int32),
            pltpu.SMEM((plan.slots,), jnp.int32),
            pltpu.SemaphoreType.DMA((8,)),
            pltpu.SemaphoreType.DMA((plan.padded,)),
        ],
        compiler_params=pltpu.CompilerParams(vmem_limit_bytes=34 << 20),
        cost_estimate=pl.CostEstimate(flops=0, bytes_accessed=1 << 16, transcendentals=0),
        name="prepare",
    )(*ints, bias, adj_one, adj_two, w_two, cot)


def call_layer_one(plan, feat_count, table, gathered, bias, adj_one, down):
    blocks = len(gathered)
    tile = adj_one.shape[-1]
    hidden = bias.shape[0]
    features = gathered[0].shape[0] * blocks
    kind = adj_one.dtype
    share = jax.ShapeDtypeStruct((feat_count // 2, 2, features // feat_count, hidden), jnp.float32)
    return pl.pallas_call(
        functools.partial(layer_one_kernel, plan, blocks),
        out_shape=(share, share, jax.ShapeDtypeStruct(down.shape, kind)),
        in_specs=[SMEM] + [VMEM] * (blocks + 3),
        out_specs=(VMEM,) * 3,
        scratch_shapes=[
            pltpu.VMEM((hidden, 2 * features), kind),
            pltpu.VMEM((2 * features, hidden), jnp.float32),
            pltpu.VMEM((2, 2 * features, BATCH * tile), kind),
            pltpu.VMEM((2, hidden, BATCH * tile), kind),
        ],
        compiler_params=pltpu.CompilerParams(vmem_limit_bytes=12 << 20),
        cost_estimate=pl.CostEstimate(
            flops=2 * plan.slots * tile * 2 * features * hidden * 3,
            bytes_accessed=20 << 20,
            transcendentals=plan.slots * tile * hidden,
        ),
        name="layer_one",
    )(table, *gathered, bias, adj_one, down)


def call_layer_two(plan, table, h_tiles, adj_two, w_two):
    own, fan, tile, _ = adj_two.shape
    hidden = w_two.shape[-1]
    kind = h_tiles.dtype
    return pl.pallas_call(
        functools.partial(layer_two_kernel, plan),
        out_shape=jax.ShapeDtypeStruct((own, tile, hidden), kind),
        in_specs=[SMEM, VMEM, VMEM, VMEM],
        out_specs=HBM,
        scratch_shapes=[
            pltpu.VMEM((own, hidden, tile), kind),
            pltpu.VMEM((own, tile, hidden), kind),
            pltpu.SemaphoreType.DMA((own,)),
        ],
        compiler_params=pltpu.CompilerParams(vmem_limit_bytes=12 << 20),
        cost_estimate=pl.CostEstimate(
            flops=2 * plan.entries * tile * tile * hidden, bytes_accessed=8 << 20, transcendentals=0
        ),
        name="layer_two",
    )(table, h_tiles, adj_two, w_two)


def body(
    x_feat,
    place,
    adj_one,
    cols_one,
    count_one,
    w_one,
    bias_one,
    adj_two,
    cols_two,
    count_two,
    w_two,
    cotangent,
):
    x_local = x_feat[0]
    feat_dev = x_local.shape[0]
    tile = adj_one.shape[-1]
    own, fan_two = adj_two.shape[1:3]
    hidden = w_two.shape[-1]
    feat_count = lax.axis_size("feat")
    plan = Plan(place.shape[1], adj_one.shape[2], own, fan_two)

    packed = jnp.concatenate([x_local, w_one[0], w_one[1]], axis=1)
    near = [packed] + [exchange(packed, "feat", m) for m in range(2, feat_count, 2)]
    far = [exchange(packed, "feat", 1)]

    ints = (place, cols_two[0], count_two, cols_one[0].T, count_one)
    down, adj_near, adj_far, weights, bias, table = call_prepare(
        plan, ints, bias_one.astype(jnp.float32).reshape(1, hidden), adj_one[0], adj_two[0], w_two, cotangent[0]
    )
    near[1:-1], down = lax.optimization_barrier((near[1:-1], down))
    far += [exchange(block, "feat", 1) for block in near[1:-1]]
    near[-1], far[1:] = lax.optimization_barrier((near[-1], far[1:]))
    far.append(exchange(near[-1], "feat", 1))
    gathered = [block for pair in zip(near, far) for block in pair]
    merge = max(1, 16 // feat_dev)
    if merge > 1:
        gathered = [
            jnp.concatenate(gathered[i : i + merge], axis=0) for i in range(0, feat_count, merge)
        ]
    even, odd, h_tiles = call_layer_one(plan, feat_count, table, gathered, bias, adj_near, down)
    layer_out = call_layer_two(plan, table, h_tiles, adj_far, weights)

    even = even + exchange(odd, "feat", 1)
    grad = even[0]
    for received in [exchange(even[j], "feat", 2 * j) for j in range(1, feat_count // 2)]:
        grad = grad + received
    level = [grad] + [exchange(grad, "grp", m) for m in range(1, lax.axis_size("grp"))]
    while len(level) > 1:
        level = [level[i] + level[i + 1] for i in range(0, len(level), 2)]
    return (layer_out.reshape(1, own * tile, hidden), level[0])


def solution(mesh):
    in_specs = (
        P("grp", "feat", None),
        P("grp", None),
        P("grp", None, None, None, None),
        P("grp", None, None),
        P("grp", None),
        P(None, "feat", None),
        P(),
        P("grp", "feat", None, None, None),
        P("grp", "feat", None),
        P("grp", "feat"),
        P(),
        P("grp", "feat", None),
    )
    out_specs = (P("grp", "feat", None), P(None, "feat", None))
    return jax.shard_map(body, mesh=mesh, in_specs=in_specs, out_specs=out_specs, check_vma=False)
```

```python
import functools

import jax
import jax.numpy as jnp
from jax import lax
from jax.experimental import pallas as pl
from jax.experimental.pallas import tpu as pltpu
from jax.sharding import PartitionSpec as P

BATCH = 4
HEAD = 8
NT = (((1,), (1,)), ((), ()))
TN = (((0,), (0,)), ((), ()))
VMEM = pl.BlockSpec(memory_space=pltpu.VMEM)
SMEM = pl.BlockSpec(memory_space=pltpu.SMEM)
HBM = pl.BlockSpec(memory_space=pltpu.HBM)


def dot(a, b, dims=(((1,), (0,)), ((), ()))):
    return lax.dot_general(a, b, dims, preferred_element_type=jnp.float32)


def exchange(array, axis, mask):
    size = lax.axis_size(axis)
    return lax.ppermute(array, axis, [(i, i ^ mask) for i in range(size)])


class Plan:
    def __init__(self, group_tiles, fan_one, own, fan_two):
        self.group_tiles, self.fan_one, self.own, self.fan_two = group_tiles, fan_one, own, fan_two
        self.entries = own * fan_two
        self.dense = self.entries == group_tiles
        self.slots = group_tiles if self.dense else self.entries + own
        self.few = fan_one // 2
        self.steps = -(-self.slots // BATCH)
        self.padded = self.steps * BATCH
        self.tile_at = HEAD
        self.slot_at = self.tile_at + self.padded + BATCH
        self.column_at = self.slot_at + self.padded + BATCH
        self.entry_at = self.column_at + (self.padded + BATCH) * fan_one
        self.table = self.entry_at + self.entries


def prepare_kernel(
    plan, place_ref, cols_two_ref, count_two_ref, cols_one_ref, count_one_ref, bias_ref,
    adj_one_ref, adj_two_ref, w_ref, cot_ref,
    d_ref, adj_one, adj_two, w_two, bias, table,
    cot, back, place, cols_two, count_two, cols_one, count_one, inverse, active, sems, adj_sems,
):
    own, fan, fan_one = plan.own, plan.fan_two, plan.fan_one
    tile = adj_two.shape[-1]
    hidden = w_two.shape[-1]
    first = lax.axis_index("feat") * own
    own_slot = first if plan.dense else plan.entries

    pairs = (
        (place_ref, place), (cols_two_ref, cols_two), (count_two_ref, count_two),
        (cols_one_ref, cols_one), (count_one_ref, count_one),
        (w_ref, w_two), (cot_ref, cot), (adj_two_ref, adj_two),
    )
    copies = [pltpu.make_async_copy(source, to, sems.at[i]) for i, (source, to) in enumerate(pairs)]
    for copy in copies:
        copy.start()
    for copy in copies[:5]:
        copy.wait()

    def adj_copy(i):
        t = table[plan.tile_at + i]
        return pltpu.make_async_copy(adj_one_ref.at[t], adj_one.at[i], adj_sems.at[i])

    @pl.loop(0, plan.group_tiles, unroll=8)
    def _(t):
        inverse[place[0, t]] = t

    @pl.loop(0, own)
    def _(p):
        count = count_two[0, p]
        for k in range(fan):
            e = p * fan + k
            slot = cols_two[p, k] if plan.dense else e
            live = k < count
            table[plan.entry_at + e] = jnp.where(live, slot, own_slot)
            if plan.dense:
                mine = jnp.logical_and(slot >= own_slot, slot < own_slot + own)
                live = jnp.logical_or(live, mine)
            active[slot] = live.astype(jnp.int32)
        if not plan.dense:
            active[plan.entries + p] = 1

    def visit(few, s, n):
        if plan.dense:
            placed = s
        else:
            e = jnp.minimum(s, plan.entries - 1)
            named = cols_two[lax.div(e, fan), lax.rem(e, fan)]
            placed = jnp.where(s < plan.entries, named, first + s - plan.entries)
        t = inverse[placed]
        table[plan.tile_at + n] = t
        table[plan.slot_at + n] = s
        count = count_one[0, t]
        fits = count <= plan.few if few else count > plan.few
        return n + jnp.where(fits, active[s], 0)

    n = lax.fori_loop(0, plan.slots, functools.partial(visit, True), jnp.int32(0), unroll=8)
    few_steps = lax.div(n, BATCH)
    n = lax.fori_loop(0, plan.slots, functools.partial(visit, False), n, unroll=8)
    steps = lax.div(n + BATCH - 1, BATCH)

    @pl.loop(n, plan.padded + BATCH)
    def _(i):
        table[plan.tile_at + i] = 0
        table[plan.slot_at + i] = plan.slots + lax.rem(i, BATCH)

    table[0] = steps
    table[1] = own_slot
    table[2] = few_steps

    @pl.loop(0, steps + 1)
    def _(step):
        for b in range(BATCH):
            i = step * BATCH + b
            t = table[plan.tile_at + i]
            for k in range(fan_one):
                table[plan.column_at + i * fan_one + k] = cols_one[k, t]

    @pl.loop(0, steps)
    def _(step):
        for b in range(BATCH):
            adj_copy(step * BATCH + b).start()

    for b in range(BATCH):
        d_ref[plan.slots + b] = jnp.zeros((hidden, tile), d_ref.dtype)
    if not plan.dense:
        for p in range(own):
            d_ref[plan.entries + p] = jnp.zeros((hidden, tile), d_ref.dtype)
    bias[...] = jnp.broadcast_to(0.5 * bias_ref[...], (tile, hidden)).T

    copies[5].wait()
    copies[6].wait()
    back[...] = dot(w_two[1], cot[...], NT).astype(back.dtype)
    copies[7].wait()

    @pl.loop(0, own)
    def _(p):
        @pl.loop(count_two[0, p], fan)
        def _(k):
            adj_two[p, k] = jnp.zeros((tile, tile), adj_two.dtype)

    for p in range(own):
        tiles = jnp.concatenate([adj_two[p, k] for k in range(fan)], axis=1)
        term = dot(back[:, p * tile : (p + 1) * tile], tiles).astype(d_ref.dtype)
        for k in range(fan):
            e = p * fan + k
            slot = cols_two[p, k] if plan.dense else e
            d_ref[slot] = term[:, k * tile : (k + 1) * tile]

    self_rows = dot(w_two[0], cot[...], NT)
    for p in range(own):
        mine = self_rows[:, p * tile : (p + 1) * tile] + d_ref[own_slot + p].astype(jnp.float32)
        d_ref[own_slot + p] = mine.astype(d_ref.dtype)

    @pl.loop(0, steps)
    def _(step):
        for b in range(BATCH):
            i = step * BATCH + b
            adj_copy(i).wait()

            @pl.loop(count_one[0, table[plan.tile_at + i]], fan_one)
            def _(k):
                adj_one[i, k] = jnp.zeros((tile, tile), adj_one.dtype)


def layer_one_kernel(plan, blocks, table, *refs):
    x_refs = refs[:blocks]
    bias, adj_one, d_ref, even_ref, odd_ref, h_ref, weight, total, both, downs = refs[blocks:]
    tile = adj_one.shape[-1]
    hidden = bias.shape[0]
    features = x_refs[0].shape[0] * blocks
    steps = table[0]

    def x_tile(t):
        at = pl.ds(pl.multiple_of(t * tile, tile), tile)
        return jnp.concatenate([x[:, at] for x in x_refs], axis=0)

    def lanes(b):
        return slice(b * tile, (b + 1) * tile)

    def aggregate(step, fan):
        at = lax.rem(step, 2)
        for b in range(BATCH):
            i = step * BATCH + b
            j = jnp.minimum(i, plan.padded - 1)
            x_all = [x_tile(table[plan.column_at + i * plan.fan_one + k]) for k in range(fan)]
            tiles = [adj_one[j, k] for k in range(fan)]
            agg = dot(jnp.concatenate(x_all, axis=1), jnp.concatenate(tiles, axis=1), NT)
            both[at, :features, lanes(b)] = x_tile(table[plan.tile_at + i])
            both[at, features:, lanes(b)] = agg.astype(both.dtype)

    def activate(step):
        at = lax.rem(step, 2)
        for b in range(0, BATCH, 2):
            z = dot(weight[...], both[at, :, b * tile : (b + 2) * tile])
            for c in range(2):
                u = z[:, lanes(c)] + bias[...]
                t = jnp.tanh(u)
                h = u * (1.0 + t)
                slope = (1.0 + t) + h * (1.0 - t)
                slot = table[plan.slot_at + step * BATCH + b + c]
                h_ref[slot] = h.astype(h_ref.dtype)
                down = d_ref[slot].astype(jnp.float32) * slope
                downs[at, :, lanes(b + c)] = down.astype(downs.dtype)

    def contract(step):
        at = lax.rem(step + 2, 2)
        total[...] += dot(both[at], downs[at], NT)

    for part in range(2):
        at = pl.ds(plan.group_tiles * tile + part * hidden, hidden)
        w = jnp.concatenate([x[:, at] for x in x_refs], axis=0)
        weight[:, part * features : (part + 1) * features] = (0.5 * w.astype(jnp.float32)).T.astype(weight.dtype)
    total[...] = jnp.zeros_like(total)
    both[1] = jnp.zeros(both.shape[1:], both.dtype)
    downs[1] = jnp.zeros(downs.shape[1:], downs.dtype)
    aggregate(0, plan.fan_one)
    turn = jnp.maximum(table[2] - 1, 0)

    @pl.loop(0, turn)
    def _(step):
        contract(step - 1)
        activate(step)
        aggregate(step + 1, plan.few)

    @pl.loop(turn, steps)
    def _(step):
        contract(step - 1)
        activate(step)
        aggregate(step + 1, plan.fan_one)

    contract(steps - 1)
    half = even_ref.shape[0]
    share = features // (2 * half)
    for m in range(2 * half):
        out = even_ref if m % 2 == 0 else odd_ref
        for part in range(2):
            at = part * features + m * share
            out[m // 2, part] = (0.5 * total[at : at + share]).astype(out.dtype)


def layer_two_kernel(plan, table, h_ref, adj_two, w_ref, out_ref, agg, out, sems):
    own, fan = plan.own, plan.fan_two
    tile = adj_two.shape[-1]
    own_slot = table[1]
    for p in range(own):
        h_all = [h_ref[table[plan.entry_at + p * fan + k]] for k in range(fan)]
        tiles = [adj_two[p, k] for k in range(fan)]
        rows = dot(jnp.concatenate(h_all, axis=1), jnp.concatenate(tiles, axis=1), NT)
        agg[p] = rows.astype(agg.dtype)
    copies = []
    for p in range(own):
        rows = dot(h_ref[own_slot + p], w_ref[0], TN) + dot(agg[p], w_ref[1], TN)
        out[p] = rows.astype(out.dtype)
        copies.append(pltpu.make_async_copy(out.at[p], out_ref.at[p], sems.at[p]))
        copies[-1].start()
    for copy in copies:
        copy.wait()


def call_prepare(plan, ints, bias, adj_one, adj_two, w_two, cot):
    adj_one, adj_two, w_two, cot, *ints = [
        pltpu.with_memory_space_constraint(a, pltpu.HBM) for a in (adj_one, adj_two, w_two, cot, *ints)
    ]
    own, fan, tile, _ = adj_two.shape
    hidden = w_two.shape[-1]
    kind = adj_one.dtype
    return pl.pallas_call(
        functools.partial(prepare_kernel, plan),
        out_shape=(
            jax.ShapeDtypeStruct((plan.slots + BATCH, hidden, tile), kind),
            jax.ShapeDtypeStruct((plan.padded, plan.fan_one, tile, tile), kind),
            jax.ShapeDtypeStruct(adj_two.shape, kind),
            jax.ShapeDtypeStruct(w_two.shape, kind),
            jax.ShapeDtypeStruct((hidden, tile), jnp.float32),
            jax.ShapeDtypeStruct((plan.table,), jnp.int32),
        ),
        in_specs=[HBM] * 5 + [VMEM] + [HBM] * 4,
        out_specs=(VMEM,) * 5 + (SMEM,),
        scratch_shapes=[
            pltpu.VMEM((own * tile, hidden), kind),
            pltpu.VMEM((hidden, own * tile), kind),
            *[pltpu.SMEM(a.shape, jnp.int32) for a in ints],
            pltpu.SMEM((plan.group_tiles,), jnp.int32),
            pltpu.SMEM((plan.slots,), jnp.int32),
            pltpu.SemaphoreType.DMA((8,)),
            pltpu.SemaphoreType.DMA((plan.padded,)),
        ],
        compiler_params=pltpu.CompilerParams(vmem_limit_bytes=34 << 20),
        cost_estimate=pl.CostEstimate(flops=0, bytes_accessed=1 << 16, transcendentals=0),
        name="prepare",
    )(*ints, bias, adj_one, adj_two, w_two, cot)


def call_layer_one(plan, feat_count, table, gathered, bias, adj_one, down):
    blocks = len(gathered)
    tile = adj_one.shape[-1]
    hidden = bias.shape[0]
    features = gathered[0].shape[0] * blocks
    kind = adj_one.dtype
    share = jax.ShapeDtypeStruct((feat_count // 2, 2, features // feat_count, hidden), jnp.float32)
    return pl.pallas_call(
        functools.partial(layer_one_kernel, plan, blocks),
        out_shape=(share, jax.ShapeDtypeStruct(share.shape, kind), jax.ShapeDtypeStruct(down.shape, kind)),
        in_specs=[SMEM] + [VMEM] * (blocks + 3),
        out_specs=(VMEM,) * 3,
        scratch_shapes=[
            pltpu.VMEM((hidden, 2 * features), kind),
            pltpu.VMEM((2 * features, hidden), jnp.float32),
            pltpu.VMEM((2, 2 * features, BATCH * tile), kind),
            pltpu.VMEM((2, hidden, BATCH * tile), kind),
        ],
        compiler_params=pltpu.CompilerParams(vmem_limit_bytes=12 << 20),
        cost_estimate=pl.CostEstimate(
            flops=2 * plan.slots * tile * 2 * features * hidden * 3,
            bytes_accessed=20 << 20,
            transcendentals=plan.slots * tile * hidden,
        ),
        name="layer_one",
    )(table, *gathered, bias, adj_one, down)


def call_layer_two(plan, table, h_tiles, adj_two, w_two):
    own, fan, tile, _ = adj_two.shape
    hidden = w_two.shape[-1]
    kind = h_tiles.dtype
    return pl.pallas_call(
        functools.partial(layer_two_kernel, plan),
        out_shape=jax.ShapeDtypeStruct((own, tile, hidden), kind),
        in_specs=[SMEM, VMEM, VMEM, VMEM],
        out_specs=HBM,
        scratch_shapes=[
            pltpu.VMEM((own, hidden, tile), kind),
            pltpu.VMEM((own, tile, hidden), kind),
            pltpu.SemaphoreType.DMA((own,)),
        ],
        compiler_params=pltpu.CompilerParams(vmem_limit_bytes=12 << 20),
        cost_estimate=pl.CostEstimate(
            flops=2 * plan.entries * tile * tile * hidden, bytes_accessed=8 << 20, transcendentals=0
        ),
        name="layer_two",
    )(table, h_tiles, adj_two, w_two)


def body(
    x_feat,
    place,
    adj_one,
    cols_one,
    count_one,
    w_one,
    bias_one,
    adj_two,
    cols_two,
    count_two,
    w_two,
    cotangent,
):
    x_local = x_feat[0]
    feat_dev = x_local.shape[0]
    tile = adj_one.shape[-1]
    own, fan_two = adj_two.shape[1:3]
    hidden = w_two.shape[-1]
    feat_count = lax.axis_size("feat")
    plan = Plan(place.shape[1], adj_one.shape[2], own, fan_two)

    packed = jnp.concatenate([x_local, w_one[0], w_one[1]], axis=1)
    near = [packed] + [exchange(packed, "feat", m) for m in range(2, feat_count, 2)]
    far = [exchange(packed, "feat", 1)]

    ints = (place, cols_two[0], count_two, cols_one[0].T, count_one)
    down, adj_near, adj_far, weights, bias, table = call_prepare(
        plan, ints, bias_one.astype(jnp.float32).reshape(1, hidden), adj_one[0], adj_two[0], w_two, cotangent[0]
    )
    near[1:-1], down = lax.optimization_barrier((near[1:-1], down))
    far += [exchange(block, "feat", 1) for block in near[1:-1]]
    near[-1], far[1:] = lax.optimization_barrier((near[-1], far[1:]))
    far.append(exchange(near[-1], "feat", 1))
    gathered = [block for pair in zip(near, far) for block in pair]
    merge = max(1, 16 // feat_dev)
    if merge > 1:
        gathered = [
            jnp.concatenate(gathered[i : i + merge], axis=0) for i in range(0, feat_count, merge)
        ]
    even, odd, h_tiles = call_layer_one(plan, feat_count, table, gathered, bias, adj_near, down)
    layer_out = call_layer_two(plan, table, h_tiles, adj_far, weights)

    even = even + exchange(odd, "feat", 1).astype(jnp.float32)
    grad = even[0]
    for received in [exchange(even[j], "feat", 2 * j) for j in range(1, feat_count // 2)]:
        grad = grad + received
    level = [grad] + [exchange(grad, "grp", m) for m in range(1, lax.axis_size("grp"))]
    while len(level) > 1:
        level = [level[i] + level[i + 1] for i in range(0, len(level), 2)]
    return (layer_out.reshape(1, own * tile, hidden), level[0])


def solution(mesh):
    in_specs = (
        P("grp", "feat", None),
        P("grp", None),
        P("grp", None, None, None, None),
        P("grp", None, None),
        P("grp", None),
        P(None, "feat", None),
        P(),
        P("grp", "feat", None, None, None),
        P("grp", "feat", None),
        P("grp", "feat"),
        P(),
        P("grp", "feat", None),
    )
    out_specs = (P("grp", "feat", None), P(None, "feat", None))
    return jax.shard_map(body, mesh=mesh, in_specs=in_specs, out_specs=out_specs, check_vma=False)
```
